32 devices in a mesh: groups: 2 (over y), space: 8 (over z, x), batch: 2 (over core).
Axes of the slice: x: 2, y: 2, z: 4, core: 2. Of those that a mesh axis runs over, the one named last changes fastest.
Arguments:
- inputs: bfloat16 [4, 8, 8, 8, 8, 1024], P(('groups', 'batch'), 'space'), parts along dimension 0, may hold values from -6 to 6
- cotangent: bfloat16 [4, 8, 8, 8, 8, 1024], P(('groups', 'batch'), 'space'), parts along dimension 0, may hold values from -6 to 6
- offsets: int32 [4], P(('groups', 'batch')), parts along dimension 0, may hold values from 1 to 7
- w_qkv: bfloat16 [1024, 3072], P('batch'), may hold values from -0.375 to 0.375
- w_out: bfloat16 [1024, 1024], P('batch'), may hold values from -0.1875 to 0.1875
- gain: float32 [1024], replicated, may hold values from 0.5 to 2, as said below
Outputs:
- update: bfloat16 [4, 8, 8, 8, 8, 1024], P(('groups', 'batch'), 'space'), parts along dimension 0
- grad: bfloat16 [4, 8, 8, 8, 8, 1024], P(('groups', 'batch'), 'space'), parts along dimension 0
The draws below stay inside these ranges and needn't reach their ends.
There are 2 independent parts, one for each index of `groups`. The reference program is written for one: setup_inputs(seed, part) draws one part's arguments, and reference() takes and returns one part's arrays. A program takes and returns all parts, laid end to end along the dimension named above; an argument that names none is the same for every part. Nothing has to cross between parts.
Inputs may be any that keep to these rules, and one draw needn't show every extreme that they name: `gain`: positive gains.
All inputs are finite; a program needn't handle non-finite values.
Results may differ from the reference program's by a relative error of at most 0.005.
The reference program's roundings to bfloat16 on the way count: a program that leaves them out, or rounds other values in their place, can miss the bound.
Values may be sent and summed in bfloat16 or wider, within the bound.
No kernel may reach another device: no remote copies, remote signals or barrier semaphores. Data moves between devices by JAX's collectives and lax.ppermute only.
A program may use at most 128 MiB of HBM per device.

```python
import jax
import jax.numpy as jnp
from jax import lax

D = 1024
WIN = 8
YTILES = 4
GZ = 8
HEAD_DIM = 64
CANDS = 2
XTILES = 2
N_SPACE = 8


def draw_gain(key, part):
    return 1.0 + 0.3 * jax.random.uniform(key, (D,), jnp.float32, -1.0, 1.0)


def level_of(own_key, extent, pieces, least, high):
    factor_of, own = 1.0, jax.random.fold_in(own_key, 6)
    for position, parts in pieces:
        heights = jnp.exp(jax.random.uniform(jax.random.fold_in(own, position), (parts,), jnp.float32, least / len(pieces), high / len(pieces)))
        factor_of = factor_of * jnp.repeat(heights, extent[position] // parts).reshape([-1 if axis == position else 1 for axis in range(len(extent))])
    return factor_of


def centred(stream_key, shape, scale, bound, shards=(), dtype=jnp.bfloat16):
    level = level_of(stream_key, shape, shards, -0.22, 0.18) if shards else 1.0
    result = jax.random.normal(stream_key, shape, jnp.float32) * scale * level
    return jnp.minimum(jnp.maximum(result, -bound), bound).astype(dtype)


def setup_inputs(seed: int = 0, part: int = 0) -> dict:
    key_list = jax.random.split(jax.random.key(seed), 7)
    part_keys = jax.random.split(jax.random.fold_in(key_list[6], part), 7)
    inputs = centred(part_keys[0], (CANDS, N_SPACE, WIN, WIN, GZ, D), 1.0, 6.0, ((0, 2), (1, 8)))
    cotangent = centred(part_keys[1], (CANDS, N_SPACE, WIN, WIN, GZ, D), 1.0, 6.0, ((0, 2), (1, 8)))
    offsets = jax.random.randint(part_keys[2], (CANDS,), 1, WIN).astype(jnp.int32)
    w_qkv = centred(key_list[3], (D, 3 * D), (D // 4) ** -0.5, 0.375, ((0, 2),))
    w_out = centred(key_list[4], (D, D), D ** -0.5, 0.1875, ((0, 2),))
    gain = draw_gain(jax.random.fold_in(key_list[6], 71), part)
    return dict(inputs=inputs, cotangent=cotangent, offsets=offsets, w_qkv=w_qkv, w_out=w_out, gain=gain)


EPS = 1e-05
GROUP_HEADS = 4

def to_windows(grid_field):
    extent_x, extent_y, extent_z, channels = grid_field.shape
    window_side = WIN
    blocks = grid_field.reshape(extent_x // window_side, window_side, extent_y // window_side, window_side, extent_z // window_side, window_side, channels)
    blocks = blocks.transpose(0, 2, 4, 1, 3, 5, 6)
    return blocks.reshape(-1, window_side * window_side * window_side, channels)

def from_windows(window_stack, extent_x, extent_y, extent_z):
    window_side = WIN
    channels = window_stack.shape[-1]
    blocks = window_stack.reshape(extent_x // window_side, extent_y // window_side, extent_z // window_side, window_side, window_side, window_side, channels)
    blocks = blocks.transpose(0, 3, 1, 4, 2, 5, 6)
    return blocks.reshape(extent_x, extent_y, extent_z, channels)

def tiles_to_grid(tiled):
    channels = tiled.shape[-1]
    blocks = tiled.reshape(XTILES, YTILES, WIN, WIN, tiled.shape[3], channels)
    return blocks.transpose(0, 2, 1, 3, 4, 5).reshape(XTILES * WIN, YTILES * WIN, tiled.shape[3], channels)

def grid_to_tiles(grid_field):
    extent_z, channels = (grid_field.shape[2], grid_field.shape[3])
    blocks = grid_field.reshape(XTILES, WIN, YTILES, WIN, extent_z, channels)
    return blocks.transpose(0, 2, 1, 3, 4, 5).reshape(XTILES * YTILES, WIN, WIN, extent_z, channels)

def split_heads(matrix):
    row_count = matrix.shape[0]
    return matrix.reshape(row_count, -1, GROUP_HEADS, HEAD_DIM).transpose(1, 0, 2, 3)

def join_heads(grouped):
    return grouped.transpose(1, 0, 2, 3).reshape(grouped.shape[1], -1)

def group_scores(query, keys):
    return jnp.einsum('qhd,khd->hqk', query.astype(jnp.float32), keys.astype(jnp.float32)) * HEAD_DIM ** (-0.5)

def probabilities(scores):
    peak = lax.optimization_barrier(jnp.max(scores, axis=-1, keepdims=True))
    raised = jnp.exp(scores - peak)
    return raised / lax.optimization_barrier(jnp.sum(raised, axis=-1, keepdims=True))

def attend_group(operands):
    query, keys, values = operands
    soft_low = probabilities(group_scores(query, keys)).astype(jnp.bfloat16)
    return jnp.einsum('hqk,khd->qhd', soft_low.astype(jnp.float32), values.astype(jnp.float32)).astype(jnp.bfloat16)

def reverse_group(operands):
    query, keys, values, upstream = operands
    soft = probabilities(group_scores(query, keys))
    grad_weights = jnp.einsum('qhd,khd->hqk', upstream.astype(jnp.float32), values.astype(jnp.float32))
    grad_scores = (soft * (grad_weights - lax.optimization_barrier(jnp.sum(grad_weights * soft, axis=-1, keepdims=True))) * HEAD_DIM ** (-0.5)).astype(jnp.bfloat16)
    grad_float = grad_scores.astype(jnp.float32)
    grad_query = jnp.einsum('hqk,khd->qhd', grad_float, keys.astype(jnp.float32)).astype(jnp.bfloat16)
    grad_keys = jnp.einsum('hqk,qhd->khd', grad_float, query.astype(jnp.float32)).astype(jnp.bfloat16)
    soft_low = soft.astype(jnp.bfloat16).astype(jnp.float32)
    grad_values = jnp.einsum('hqk,qhd->khd', soft_low, upstream.astype(jnp.float32)).astype(jnp.bfloat16)
    return (grad_query, grad_keys, grad_values)

def window_block(tokens, cot_tokens, w_qkv, w_out, gain):
    channels = tokens.shape[1]
    values32 = tokens.astype(jnp.float32)
    center = values32 - lax.optimization_barrier(jnp.mean(values32, axis=-1, keepdims=True))
    inverse = lax.rsqrt(lax.optimization_barrier(jnp.mean(center * center, axis=-1, keepdims=True)) + EPS)
    normed = center * inverse
    scaled = (normed * gain).astype(jnp.bfloat16)
    projected = jnp.dot(scaled, w_qkv, preferred_element_type=jnp.float32)
    query = projected[:, :channels].astype(jnp.bfloat16)
    keys = projected[:, channels:2 * channels].astype(jnp.bfloat16)
    values = projected[:, 2 * channels:].astype(jnp.bfloat16)
    grouped = (split_heads(query), split_heads(keys), split_heads(values))
    attended = join_heads(lax.map(attend_group, grouped))
    frame_update = jnp.dot(attended, w_out, preferred_element_type=jnp.float32).astype(jnp.bfloat16)
    upstream = jnp.dot(cot_tokens, w_out.T, preferred_element_type=jnp.float32).astype(jnp.bfloat16)
    grad_query, grad_keys, grad_values = lax.map(reverse_group, grouped + (split_heads(upstream),))
    grad_qkv = jnp.concatenate([join_heads(grad_query), join_heads(grad_keys), join_heads(grad_values)], axis=1)
    grad_normed = jnp.dot(grad_qkv, w_qkv.T, preferred_element_type=jnp.float32) * gain
    mean_grad = lax.optimization_barrier(jnp.mean(grad_normed, axis=-1, keepdims=True))
    mean_mixed = lax.optimization_barrier(jnp.mean(grad_normed * normed, axis=-1, keepdims=True))
    frame_grad = (inverse * (grad_normed - mean_grad - normed * mean_mixed)).astype(jnp.bfloat16)
    return (frame_update, frame_grad)

def reference(inputs, cotangent, offsets, w_qkv, w_out, gain):

    def candidate(operands):
        tiled_in, tiled_cot, start = operands
        grid_in = tiles_to_grid(tiled_in)
        grid_cot = tiles_to_grid(tiled_cot)
        extent_x, extent_y, extent_z = (grid_in.shape[0], grid_in.shape[1], grid_in.shape[2])
        rolled_in = to_windows(jnp.roll(grid_in, -start, axis=0))
        rolled_cot = to_windows(jnp.roll(grid_cot, -start, axis=0))

        def one_window(pair):
            return window_block(pair[0], pair[1], w_qkv, w_out, gain)
        updates, grads = lax.map(one_window, (rolled_in, rolled_cot))
        update_grid = jnp.roll(from_windows(updates, extent_x, extent_y, extent_z), start, axis=0)
        grad_grid = jnp.roll(from_windows(grads, extent_x, extent_y, extent_z), start, axis=0)
        return (grid_to_tiles(update_grid), grid_to_tiles(grad_grid))
    update, grad = lax.map(candidate, (inputs, cotangent, offsets.astype(jnp.int32)))
    return (update, grad)
```

```python
import functools

import jax
import jax.numpy as jnp
from jax import lax
from jax.experimental import pallas as pl
from jax.experimental.pallas import tpu as pltpu
from jax.sharding import PartitionSpec as P

WIN = 8
YTILES = 4
HEAD_DIM = 64
EPS = 1e-05
PAIR = 2 * HEAD_DIM
QUAD = 4 * HEAD_DIM
HALF_WIN = WIN // 2
LEAD = 2
BF16 = jnp.bfloat16
F32 = jnp.float32
ANYWHERE = pl.BlockSpec(memory_space=pl.ANY)


def dot(left, right, left_dim, right_dim):
    return lax.dot_general(
        left, right, (((left_dim,), (right_dim,)), ((), ())), preferred_element_type=F32
    )


def normalise(tokens):
    values32 = tokens.astype(F32)
    center = values32 - jnp.mean(values32, axis=-1, keepdims=True)
    inverse = lax.rsqrt(jnp.mean(center * center, axis=-1, keepdims=True) + EPS)
    return center * inverse, inverse


def norm_backward(tokens, grad_scaled, gain):
    normed, inverse = normalise(tokens)
    grad_normed = grad_scaled * gain
    mean_grad = jnp.mean(grad_normed, axis=-1, keepdims=True)
    mean_mixed = jnp.mean(grad_normed * normed, axis=-1, keepdims=True)
    return (inverse * (grad_normed - mean_grad - normed * mean_mixed)).astype(BF16)


def head_mask(pair, head):
    lane = lax.broadcasted_iota(jnp.int32, pair.shape, 1)
    return jnp.where((lane < HEAD_DIM) == (head == 0), pair, jnp.zeros_like(pair))


def aligned(value, multiple):
    return pl.multiple_of(value, multiple)


def call(kernel, name, grid, in_specs, out_specs, out_shape, scratch, flops, scalars=1, aliases=None):
    return pl.pallas_call(
        kernel,
        grid_spec=pltpu.PrefetchScalarGridSpec(
            num_scalar_prefetch=scalars,
            grid=grid,
            in_specs=in_specs,
            out_specs=out_specs,
            scratch_shapes=scratch,
        ),
        out_shape=out_shape,
        compiler_params=pltpu.CompilerParams(vmem_limit_bytes=59 << 20),
        cost_estimate=pl.CostEstimate(flops=flops, bytes_accessed=20 << 20, transcendentals=0),
        input_output_aliases=aliases or {},
        name=name,
    )


def whole(*_):
    return (0, 0)


BATCH, SLOT, FIRST, OTHERS, EXTRA, ODD = range(6)


def scale_into(scaled, rows, tokens, gain, batch):
    normed, _ = normalise(tokens)
    values = (normed * gain).astype(BF16)
    half = values.shape[1] // 2
    near, far = values[:, :half], values[:, half:]
    scaled[rows, :half] = jnp.where(batch == 0, near, far)
    scaled[rows, half:] = jnp.where(batch == 0, far, near)


def gather_rows(batch, here, there, full, sems):
    half = here.shape[0]
    return (
        pltpu.make_async_copy(here, full.at[pl.ds(aligned(batch * half, half), half)], sems.at[0]),
        pltpu.make_async_copy(there, full.at[pl.ds(aligned((1 - batch) * half, half), half)], sems.at[1]),
    )


def own_kernel(
    meta, tokens, gain, w_here, w_there, cot, o_here, o_there, qkv, upstream,
    scaled, cot_copy, o_full, sems,
):
    step = pl.program_id(0)
    batch = meta[BATCH]
    half = w_here.shape[0]
    copies = (pltpu.make_async_copy(cot, cot_copy, sems.at[2]),) + gather_rows(
        batch, o_here, o_there, o_full, sems
    )

    @pl.when(step == 0)
    def _():
        for copy in copies:
            copy.start()
        scale_into(scaled, slice(None), tokens[...], gain[...], batch)

    qkv[...] = (
        dot(scaled[:, :half], w_here[...], 1, 0) + dot(scaled[:, half:], w_there[...], 1, 0)
    ).astype(BF16)

    @pl.when(step == pl.num_programs(0) - 1)
    def _():
        for copy in copies:
            copy.wait()

        def columns(index, carry):
            at = pl.ds(aligned(index * QUAD, QUAD), QUAD)
            upstream[:, at] = dot(cot_copy[...], o_full[at, :], 1, 1).astype(BF16)
            return carry

        lax.fori_loop(0, upstream.shape[1] // QUAD, columns, 0)


def own_projection(meta, tokens, gain, w_here, w_there, cot, o_here, o_there):
    rows, channels = tokens.shape
    half, width = w_here.shape
    chunk = 512
    return call(
        own_kernel,
        "own_projection",
        (width // chunk,),
        [pl.BlockSpec((rows, channels), whole), pl.BlockSpec((1, channels), whole)]
        + [pl.BlockSpec((half, chunk), lambda i, _: (0, i))] * 2
        + [ANYWHERE] * 3,
        [pl.BlockSpec((rows, chunk), lambda i, _: (0, i)), pl.BlockSpec((rows, channels), whole)],
        [jax.ShapeDtypeStruct((rows, width), BF16), jax.ShapeDtypeStruct((rows, channels), BF16)],
        [
            pltpu.VMEM((rows, channels), BF16),
            pltpu.VMEM((rows, channels), BF16),
            pltpu.VMEM((channels, channels), BF16),
            pltpu.SemaphoreType.DMA((3,)),
        ],
        2 * rows * channels * (width + channels),
    )(meta, tokens, gain, w_here, w_there, cot, o_here, o_there)


def forward_kernel(
    meta, *refs, parts,
):
    received, refs = refs[:parts], refs[parts:]
    (
        gain, q_own, k_own, v_own, q_here, k_here, v_here, q_there, k_there, v_there, o_here, o_there,
        q_out, k_out, v_out, probs_out, att_out, update_out, x_out,
        scaled, attended, o_full, sems,
    ) = refs
    step = pl.program_id(0)
    batch = meta[BATCH]
    half = q_here.shape[0]
    count = scaled.shape[0]
    lead = received[0].shape[0]
    first = pl.ds(aligned(meta[FIRST], HEAD_DIM), lead)
    others = pl.ds(aligned(meta[OTHERS], HEAD_DIM), count - lead)
    extra = pl.ds(aligned(meta[EXTRA], HEAD_DIM), HEAD_DIM)
    slot = aligned(meta[SLOT], HEAD_DIM)
    copies = gather_rows(batch, o_here, o_there, o_full, sems)

    @pl.when(step == 0)
    def _():
        for copy in copies:
            copy.start()
        scale_into(scaled, slice(0, lead), received[0][...], gain[...], batch)
        x_out[pl.ds(aligned(meta[FIRST] - slot, HEAD_DIM), lead), :] = received[0][...]
        if parts > 1:
            scale_into(scaled, slice(lead, count), received[1][...], gain[...], batch)
            x_out[pl.ds(aligned(meta[OTHERS] - slot, HEAD_DIM), count - lead), :] = received[1][...]

    for own, here, there, out in (
        (q_own, q_here, q_there, q_out),
        (k_own, k_here, k_there, k_out),
        (v_own, v_here, v_there, v_out),
    ):
        out[...] = own[...]
        fresh = (dot(scaled[:, :half], here[...], 1, 0) + dot(scaled[:, half:], there[...], 1, 0)).astype(BF16)
        out[first, :] = fresh[:lead]
        if parts > 1:
            out[others, :] = fresh[lead:]

        @pl.when(meta[ODD] == 1)
        def _():
            out[extra, :] = own[extra, :]

    def pair_of_heads(pair, carry):
        columns = pl.ds(aligned(pair * PAIR, PAIR), PAIR)
        query = q_out[:, columns] * BF16(HEAD_DIM ** -0.5)
        keys = k_out[:, columns]
        values_t = v_out[:, columns].T
        outs = []
        for head in range(2):
            scores = dot(keys, head_mask(query, head), 1, 1)
            peak = jnp.max(scores, axis=0, keepdims=True)
            raised = jnp.exp(scores - peak)
            total = jnp.sum(raised, axis=0, keepdims=True)
            probs = raised * (1.0 / total)
            probs_out[2 * pair + head] = probs
            rows = slice(HEAD_DIM * head, HEAD_DIM * head + HEAD_DIM)
            outs.append(dot(values_t[rows], probs.astype(BF16), 1, 0))
        block = jnp.concatenate(outs, axis=0).astype(BF16).T
        att_out[:, columns] = block
        attended[:, pl.ds(aligned(step * QUAD + pair * PAIR, PAIR), PAIR)] = block
        return carry

    lax.fori_loop(0, QUAD // PAIR, pair_of_heads, 0)

    @pl.when(step == pl.num_programs(0) - 1)
    def _():
        for copy in copies:
            copy.wait()

        def columns(index, carry):
            at = pl.ds(aligned(index * QUAD, QUAD), QUAD)
            update_out[:, at] = dot(attended[pl.ds(slot, count), :], o_full[:, at], 1, 0).astype(BF16)
            return carry

        lax.fori_loop(0, update_out.shape[1] // QUAD, columns, 0)


def forward(meta, received, gain, qkv, w_here, w_there, o_here, o_there):
    rows = qkv.shape[0]
    half, channels = o_here.shape
    count = sum(part.shape[0] for part in received)
    quads = channels // QUAD

    def column(part):
        return lambda i, _: (0, i + part * quads)

    block = jax.ShapeDtypeStruct((rows, channels), BF16)
    block_spec = pl.BlockSpec((rows, QUAD), column(0))
    moved = jax.ShapeDtypeStruct((count, channels), BF16)
    weights = [pl.BlockSpec((half, QUAD), column(part)) for part in range(3)]
    return call(
        functools.partial(forward_kernel, parts=len(received)),
        "forward",
        (quads,),
        [pl.BlockSpec(part.shape, whole) for part in received]
        + [pl.BlockSpec((1, channels), whole)]
        + [pl.BlockSpec((rows, QUAD), column(part)) for part in range(3)]
        + weights * 2
        + [ANYWHERE] * 2,
        [block_spec] * 3
        + [pl.BlockSpec((QUAD // HEAD_DIM, rows, rows), lambda i, _: (i, 0, 0)), block_spec]
        + [pl.BlockSpec((count, channels), whole)] * 2,
        [block] * 3
        + [jax.ShapeDtypeStruct((channels // HEAD_DIM, rows, rows), F32), block, moved, moved],
        [
            pltpu.VMEM((count, channels), BF16),
            pltpu.VMEM((rows, channels), BF16),
            pltpu.VMEM((channels, channels), BF16),
            pltpu.SemaphoreType.DMA((2,)),
        ],
        12 * 10 ** 9,
    )(meta, *received, gain, qkv, qkv, qkv, *[w_here] * 3, *[w_there] * 3, o_here, o_there)


def backward_kernel(
    meta, x_slot, c_slot, gain, query, keys, values, probs, u_own, o_here, o_there, w_here, w_there,
    dq_out, dk_out, dv_out, grad_out,
    upstream, grad_qkv, w_full, back, sems,
):
    step = pl.program_id(0)
    batch = meta[BATCH]
    count, channels = grad_out.shape
    slot = pl.ds(aligned(meta[SLOT], HEAD_DIM), count)
    extra = pl.ds(aligned(meta[EXTRA], HEAD_DIM), HEAD_DIM)
    copies = gather_rows(batch, w_here, w_there, w_full, sems)

    @pl.when(step == 0)
    def _():
        for copy in copies:
            copy.start()

    upstream[...] = u_own[...]
    here = step // 2 == batch
    w_rows = jnp.where(here, o_here[...], o_there[...])
    upstream[slot, :] = dot(c_slot[...], w_rows, 1, 1).astype(BF16)

    @pl.when(meta[ODD] == 1)
    def _():
        upstream[extra, :] = u_own[extra, :]

    scale = HEAD_DIM ** -0.5

    def pair_of_heads(pair, carry):
        columns = pl.ds(aligned(pair * PAIR, PAIR), PAIR)
        pair_query = query[:, columns]
        pair_keys_t = keys[:, columns].T
        pair_values = values[:, columns]
        pair_up = upstream[:, columns]
        grad_keys = None
        grad_values = None
        outs = []
        for head in range(2):
            soft = probs[2 * pair + head]
            grad_probs = dot(head_mask(pair_values, head), pair_up, 1, 1)
            mixed = grad_probs * soft
            row_sum = jnp.sum(mixed, axis=0, keepdims=True)
            grad_scores = (mixed - soft * row_sum).astype(BF16)
            rows = slice(HEAD_DIM * head, HEAD_DIM * head + HEAD_DIM)
            outs.append(dot(pair_keys_t[rows], grad_scores, 1, 0))
            from_keys = dot(grad_scores, head_mask(pair_query, head), 1, 0)
            from_values = dot(soft.astype(BF16), head_mask(pair_up, head), 1, 0)
            grad_keys = from_keys if head == 0 else grad_keys + from_keys
            grad_values = from_values if head == 0 else grad_values + from_values
        blocks = (
            (jnp.concatenate(outs, axis=0) * scale).astype(BF16).T,
            (grad_keys * scale).astype(BF16),
            grad_values.astype(BF16),
        )
        for part, (out, block) in enumerate(zip((dq_out, dk_out, dv_out), blocks)):
            out[:, columns] = block
            grad_qkv[:, pl.ds(aligned(part * channels + step * QUAD + pair * PAIR, PAIR), PAIR)] = block
        return carry

    lax.fori_loop(0, QUAD // PAIR, pair_of_heads, 0)

    @pl.when(step == pl.num_programs(0) - 1)
    def _():
        for copy in copies:
            copy.wait()

        def columns(index, carry):
            at = pl.ds(aligned(index * QUAD, QUAD), QUAD)
            back[:, at] = dot(grad_qkv[slot, :], w_full[at, :], 1, 1)
            return carry

        lax.fori_loop(0, channels // QUAD, columns, 0)
        grad_out[...] = norm_backward(x_slot[...], back[...], gain[...])


def backward(meta, x_slot, c_slot, gain, query, keys, values, probs, u_own, o_here, o_there, w_here, w_there):
    rows, channels = query.shape
    count = x_slot.shape[0]
    quads = channels // QUAD

    def column(i, _):
        return (0, i)

    def here(i, meta):
        return (jnp.clip(i - 2 * meta[BATCH], 0, 1), 0)

    def there(i, meta):
        return (jnp.clip(i - 2 * (1 - meta[BATCH]), 0, 1), 0)

    block = jax.ShapeDtypeStruct((rows, channels), BF16)
    block_spec = pl.BlockSpec((rows, QUAD), column)
    return call(
        backward_kernel,
        "backward",
        (quads,),
        [pl.BlockSpec((count, channels), whole)] * 2
        + [pl.BlockSpec((1, channels), whole)]
        + [block_spec] * 3
        + [pl.BlockSpec((QUAD // HEAD_DIM, rows, rows), lambda i, _: (i, 0, 0)), block_spec]
        + [pl.BlockSpec((QUAD, channels), here), pl.BlockSpec((QUAD, channels), there)]
        + [ANYWHERE] * 2,
        [block_spec] * 3 + [pl.BlockSpec((count, channels), whole)],
        [block] * 3 + [jax.ShapeDtypeStruct((count, channels), BF16)],
        [
            pltpu.VMEM((rows, QUAD), BF16),
            pltpu.VMEM((rows, 3 * channels), BF16),
            pltpu.VMEM((channels, 3 * channels), BF16),
            pltpu.VMEM((count, channels), F32),
            pltpu.SemaphoreType.DMA((2,)),
        ],
        20 * 10 ** 9,
    )(meta, x_slot, c_slot, gain, query, keys, values, probs, u_own, o_here, o_there, w_here, w_there)


def finish_kernel(
    meta, tokens, gain, attended, dq, dk, dv, o_here, o_there, w_here, w_there, received,
    update_out, grad_out,
    o_full, w_full, back, o_sems, w_sems,
):
    step = pl.program_id(0)
    batch = meta[BATCH]
    channels = tokens.shape[1]
    o_copies = gather_rows(batch, o_here, o_there, o_full, o_sems)
    w_copies = gather_rows(batch, w_here, w_there, w_full, w_sems)

    @pl.when(step == 0)
    def _():
        for copy in o_copies + w_copies:
            copy.start()
        for copy in o_copies + w_copies:
            copy.wait()

    def columns(index, carry):
        at = pl.ds(aligned(index * QUAD, QUAD), QUAD)
        update_out[:, at] = dot(attended[...], o_full[:, at], 1, 0).astype(BF16)
        total = dot(dq[...], w_full[at, :channels], 1, 1)
        total = total + dot(dk[...], w_full[at, channels : 2 * channels], 1, 1)
        back[:, at] = total + dot(dv[...], w_full[at, 2 * channels :], 1, 1)
        return carry

    lax.fori_loop(0, channels // QUAD, columns, 0)
    grad_out[...] = norm_backward(tokens[...], back[...], gain[...])


def finish(meta, tokens, gain, attended, dq, dk, dv, o_here, o_there, w_here, w_there, received):
    rows, channels = tokens.shape
    chunk = 256
    block = jax.ShapeDtypeStruct((rows, channels), BF16)
    spec = pl.BlockSpec((chunk, channels), lambda i, _: (i, 0))
    return call(
        finish_kernel,
        "finish",
        (rows // chunk,),
        [spec, pl.BlockSpec((1, channels), whole)] + [spec] * 4 + [ANYWHERE] * 5,
        [spec] * 2,
        [block] * 2,
        [
            pltpu.VMEM((channels, channels), BF16),
            pltpu.VMEM((channels, 3 * channels), BF16),
            pltpu.VMEM((chunk, channels), F32),
            pltpu.SemaphoreType.DMA((2,)),
            pltpu.SemaphoreType.DMA((2,)),
        ],
        8 * rows * channels * channels,
    )(meta, tokens, gain, attended, dq, dk, dv, o_here, o_there, w_here, w_there, received)


def merge_kernel(meta, update_back, grad_back, update, grad, update_out, grad_out):
    own = (meta[ODD] == 1) & (meta[SLOT] + pl.program_id(0) * update_out.shape[0] == meta[EXTRA])
    update_out[...] = jnp.where(own, update[...], update_back[...])
    grad_out[...] = jnp.where(own, grad[...], grad_back[...])


def merge(meta, update_back, grad_back, update, grad):
    count, channels = update_back.shape
    row = WIN * WIN
    piece = pl.BlockSpec((row, channels), lambda i, _: (i, 0))
    place = pl.BlockSpec((row, channels), lambda i, meta: (meta[SLOT] // row + i, 0))
    block = jax.ShapeDtypeStruct(update.shape, BF16)
    return call(
        merge_kernel, "merge", (count // row,), [piece] * 2 + [place] * 2, [place] * 2, [block] * 2, [],
        0, aliases={3: 0, 4: 1},
    )(meta, update_back, grad_back, update, grad)


def take_kernel(meta, source, earlier, out):
    out[...] = source[...]


def take(meta, source, count, earlier):
    channels = source.shape[1]
    row = WIN * WIN
    return call(
        take_kernel,
        "take",
        (count // row,),
        [pl.BlockSpec((row, channels), lambda i, meta: (meta[SLOT] // row + i, 0)), ANYWHERE],
        pl.BlockSpec((row, channels), lambda i, _: (i, 0)),
        jax.ShapeDtypeStruct((count, channels), BF16),
        [],
        0,
    )(meta, source, earlier)


def exchange(rows, near, back):
    size = lax.axis_size("space")

    def along(by):
        return lax.ppermute(rows, "space", [(i, (i + by) % size) for i in range(size)])

    if size == 2 * YTILES:
        return along(YTILES)
    return jnp.where(near != back, along(-YTILES), along(YTILES))


def swapped(part):
    return lax.ppermute(part, "batch", [(0, 1), (1, 0)])


def shards(inputs, cotangent, offsets, w_qkv, w_out, gain):
    tiled_shape = inputs.shape
    channels = tiled_shape[-1]
    row = WIN * tiled_shape[4]
    tokens = inputs.reshape(-1, channels)
    cot = cotangent.reshape(-1, channels)
    gain = gain.reshape(1, channels)
    shift = offsets[0]
    near = shift <= HALF_WIN
    moved = jnp.minimum(shift, WIN - shift)
    batch = lax.axis_index("batch")

    first = jnp.where(near, 0, (WIN - LEAD) * row)
    o_there = swapped(w_out)
    w_there = swapped(w_qkv)
    x_first = exchange(lax.dynamic_slice_in_dim(tokens, first, LEAD * row, 0), near, False)

    def meta_of(count):
        slot = jnp.where(near, 0, (WIN - count) * row)
        others = jnp.where(near, LEAD * row, (WIN - count) * row)
        extra = jnp.where(near, (count - 1) * row, (WIN - count) * row)
        return jnp.stack([batch, slot, first, others, extra, moved % 2]).astype(jnp.int32)

    qkv, u_own = own_projection(meta_of(LEAD), tokens, gain, w_qkv, w_there, cot, w_out, o_there)

    def branch(count):
        def run(tokens, cot, x_first, qkv, u_own, w_qkv, w_there, w_out, o_there):
            meta = meta_of(count)
            if count > LEAD:
                x_others = exchange(
                    lax.dynamic_slice_in_dim(tokens, meta[OTHERS], (count - LEAD) * row, 0), near, False
                )
                received = (x_first, x_others)
                c_sent = take(meta, cot, count * row, x_others)
            else:
                received = (x_first,)
                c_sent = lax.dynamic_slice_in_dim(cot, meta[SLOT], count * row, 0)
            c_slot = exchange(c_sent, near, False)
            query, keys, values, probs, attended, update_sent, x_slot = forward(
                meta, received, gain, qkv, w_qkv, w_there, w_out, o_there
            )
            update_back = exchange(update_sent, near, True)
            dq, dk, dv, grad_sent = backward(
                meta, x_slot, c_slot, gain, query, keys, values, probs, u_own, w_out, o_there, w_qkv, w_there
            )
            grad_back = exchange(grad_sent, near, True)
            update, grad = finish(
                meta, tokens, gain, attended, dq, dk, dv, w_out, o_there, w_qkv, w_there, update_back
            )
            return merge(meta, update_back, grad_back, update, grad)

        return run

    update, grad = lax.cond(
        moved <= LEAD, branch(LEAD), branch(HALF_WIN),
        tokens, cot, x_first, qkv, u_own, w_qkv, w_there, w_out, o_there,
    )
    return (update.reshape(tiled_shape), grad.reshape(tiled_shape))


def solution(mesh):
    in_specs = (
        P(("groups", "batch"), "space", None, None, None, None),
        P(("groups", "batch"), "space", None, None, None, None),
        P(("groups", "batch")),
        P("batch", None),
        P("batch", None),
        P(),
    )
    out_specs = (
        P(("groups", "batch"), "space", None, None, None, None),
        P(("groups", "batch"), "space", None, None, None, None),
    )
    return jax.shard_map(shards, mesh=mesh, in_specs=in_specs, out_specs=out_specs, check_vma=False)
```

```python
import functools

import jax
import jax.numpy as jnp
from jax import lax
from jax.experimental import pallas as pl
from jax.experimental.pallas import tpu as pltpu
from jax.sharding import PartitionSpec as P

WIN = 8
YTILES = 4
HEAD_DIM = 64
EPS = 1e-05
PAIR = 2 * HEAD_DIM
QUAD = 4 * HEAD_DIM
HALF_WIN = WIN // 2
LEAD = 2
BF16 = jnp.bfloat16
F32 = jnp.float32
NORM_ROWS = 64
ROW_CHUNK = 64
PIECES = 4
ANYWHERE = pl.BlockSpec(memory_space=pltpu.HBM)
VECTOR = pl.BlockSpec(memory_space=pltpu.VMEM)
SCALAR = pl.BlockSpec(memory_space=pltpu.SMEM)
NORM_ROWS = 64
ROW_CHUNK = 64
PIECES = 4
PAIRS_AT_ONCE = 1


def dot(left, right, left_dim, right_dim):
    return lax.dot_general(
        left, right, (((left_dim,), (right_dim,)), ((), ())), preferred_element_type=F32
    )


def normalise(tokens):
    values32 = tokens.astype(F32)
    center = values32 - jnp.mean(values32, axis=-1, keepdims=True)
    inverse = lax.rsqrt(jnp.mean(center * center, axis=-1, keepdims=True) + EPS)
    return center * inverse, inverse


def norm_backward(tokens, grad_scaled, gain):
    normed, inverse = normalise(tokens)
    grad_normed = grad_scaled * gain
    mean_grad = jnp.mean(grad_normed, axis=-1, keepdims=True)
    mean_mixed = jnp.mean(grad_normed * normed, axis=-1, keepdims=True)
    return (inverse * (grad_normed - mean_grad - normed * mean_mixed)).astype(BF16)


def head_mask(pair, head):
    lane = lax.broadcasted_iota(jnp.int32, pair.shape, 1)
    return jnp.where((lane < HEAD_DIM) == (head == 0), pair, jnp.zeros_like(pair))


def aligned(value, multiple):
    return pl.multiple_of(value, multiple)


def span(start, size):
    return pl.ds(aligned(start, size), size)


def call(kernel, name, in_specs, out_specs, out_shape, scratch, mib, flops, aliases=None):
    return pl.pallas_call(
        kernel,
        in_specs=in_specs,
        out_specs=out_specs,
        out_shape=out_shape,
        scratch_shapes=scratch,
        compiler_params=pltpu.CompilerParams(vmem_limit_bytes=mib << 20),
        cost_estimate=pl.CostEstimate(flops=flops, bytes_accessed=1 << 20, transcendentals=0),
        input_output_aliases=aliases or {},
        name=name,
    )


BATCH, SLOT, FIRST, OTHERS, EXTRA, ODD = range(6)


def over_rows(count, body):
    def step(index, carry):
        body(span(index * NORM_ROWS, NORM_ROWS))
        return carry

    lax.fori_loop(0, count // NORM_ROWS, step, 0)


def shifted(rows, by):
    return pl.ds(aligned(rows.start + by, HEAD_DIM), rows.size)


def scale_rows(batch, tokens, gain, scaled, into=0):
    half = tokens.shape[1] // 2

    def body(rows):
        normed, _ = normalise(tokens[rows, :])
        values = (normed * gain[...]).astype(BF16)
        place = shifted(rows, into)
        scaled[place, :half] = jnp.where(batch == 0, values[:, :half], values[:, half:])
        scaled[place, half:] = jnp.where(batch == 0, values[:, half:], values[:, :half])

    over_rows(tokens.shape[0], body)


def norm_backward_rows(tokens, back, gain, out, at=0):
    def body(rows):
        place = shifted(rows, at)
        out[place, :] = norm_backward(tokens[rows, :], back[place, :], gain[...])

    over_rows(tokens.shape[0], body)


def times_rows(batch, left, weights, out, rows, chunk):
    half = weights.shape[0] // 2
    per_half = half // chunk

    def columns(index, carry):
        place = jnp.where(index < per_half, batch, 1 - batch) * half + lax.rem(index, per_half) * chunk
        product = dot(left(), weights[span(index * chunk, chunk), :], 1, 1)
        out[rows, span(place, chunk)] = product.astype(out.dtype)
        return carry

    lax.fori_loop(0, 2 * per_half, columns, 0)


def times_halves(batch, left, rows, weights, out, chunk):
    half = weights.shape[0] // 2

    def columns(index, carry):
        at = span(index * chunk, chunk)
        product = dot(left[rows, span(batch * half, half)], weights[:half, at], 1, 0)
        product = product + dot(left[rows, span((1 - batch) * half, half)], weights[half:, at], 1, 0)
        out[:, at] = product.astype(BF16)
        return carry

    lax.fori_loop(0, weights.shape[1] // chunk, columns, 0)


def weight_rows(here, there, full, sems):
    half = here.shape[0]
    size = half // PIECES
    return tuple(
        pltpu.make_async_copy(
            source.at[pl.ds(piece * size, size)],
            full.at[pl.ds(place * half + piece * size, size)],
            sems.at[place * PIECES + piece],
        )
        for place, source in enumerate((here, there))
        for piece in range(PIECES)
    )


def multiply_columns(tokens, weights, out):
    def columns(index, carry):
        at = span(index * QUAD, QUAD)
        out[:, at] = dot(tokens[...], weights[at, :], 1, 1).astype(BF16)
        return carry

    lax.fori_loop(0, weights.shape[0] // QUAD, columns, 0)


def own_kernel(meta, tokens, cot, gain, o_here, scaled, upstream, x_sent, c_sent, c_sent_few):
    scale_rows(meta[BATCH], tokens, gain, scaled)
    multiply_columns(cot, o_here, upstream)
    near = meta[SLOT] == 0
    few = c_sent_few.shape[0]
    x_sent[...] = tokens[pl.ds(aligned(jnp.where(near, LEAD * HEAD_DIM, HALF_WIN * HEAD_DIM), HEAD_DIM), few), :]
    c_sent[...] = cot[pl.ds(aligned(jnp.where(near, 0, HALF_WIN * HEAD_DIM), HEAD_DIM), 2 * few), :]
    c_sent_few[...] = cot[pl.ds(aligned(meta[SLOT], HEAD_DIM), few), :]


def own_tokens(meta, tokens, cot, gain, o_here):
    rows, channels = tokens.shape
    half = o_here.shape[0]
    few = LEAD * HEAD_DIM
    shapes = [(rows, channels), (rows, half), (few, channels), (2 * few, channels), (few, channels)]
    return call(
        own_kernel,
        "own_tokens",
        [SCALAR] + [VECTOR] * 4,
        [VECTOR] * 5,
        [jax.ShapeDtypeStruct(shape, BF16) for shape in shapes],
        [],
        10,
        rows * channels * channels,
    )(meta, tokens, cot, gain, o_here)


def rest_kernel(
    meta, x_first, gain, scaled_in, cot_in, w_here, w_there, o_there, qkv, upstream,
    scaled, cot, w_full, o_rows, sems, w_sems,
):
    half, width = w_here.shape
    rows = qkv.shape[0]
    first = pl.ds(aligned(meta[FIRST], HEAD_DIM), x_first.shape[0])
    extra = pl.ds(aligned(meta[EXTRA], HEAD_DIM), HEAD_DIM)
    chunk = 512
    chunks = width // chunk
    scaled_copy = pltpu.make_async_copy(scaled_in, scaled.at[pl.ds(0, rows)], sems.at[0])
    later = (
        pltpu.make_async_copy(cot_in, cot, sems.at[1]),
        pltpu.make_async_copy(o_there, o_rows, sems.at[2]),
    )

    def weight_copies(index):
        at = pl.ds(aligned(index * chunk, chunk), chunk)
        return (
            pltpu.make_async_copy(w_here.at[:, at], w_full.at[pl.ds(0, half), at], w_sems.at[0, index]),
            pltpu.make_async_copy(w_there.at[:, at], w_full.at[pl.ds(half, half), at], w_sems.at[1, index]),
        )

    scaled_copy.start()

    def start_weights(index, carry):
        for copy in weight_copies(index):
            copy.start()
        return carry

    lax.fori_loop(0, chunks, start_weights, 0)
    for copy in later:
        copy.start()
    scale_rows(meta[BATCH], x_first, gain, scaled, rows)
    scaled_copy.wait()

    def project(index, carry):
        for copy in weight_copies(index):
            copy.wait()
        at = pl.ds(aligned(index * chunk, chunk), chunk)
        product = dot(scaled[...], w_full[:, at], 1, 0).astype(BF16)
        qkv[:, at] = product[:rows]
        own = qkv[extra, at]
        qkv[first, at] = product[rows:]

        @pl.when(meta[ODD] == 1)
        def _():
            qkv[extra, at] = own

        return carry

    lax.fori_loop(0, chunks, project, 0)
    for copy in later:
        copy.wait()
    multiply_columns(cot, o_rows, upstream)


def rest_projection(meta, x_first, gain, scaled, cot, w_here, w_there, o_there):
    rows, channels = scaled.shape
    half, width = w_there.shape
    return call(
        rest_kernel,
        "rest_projection",
        [SCALAR] + [VECTOR] * 2 + [ANYWHERE] * 5,
        [VECTOR] * 2,
        [jax.ShapeDtypeStruct((rows, width), BF16), jax.ShapeDtypeStruct((rows, half), BF16)],
        [
            pltpu.VMEM((rows + x_first.shape[0], channels), BF16),
            pltpu.VMEM((rows, channels), BF16),
            pltpu.VMEM((channels, width), BF16),
            pltpu.VMEM((half, channels), BF16),
            pltpu.SemaphoreType.DMA((3,)),
            pltpu.SemaphoreType.DMA((2, width // 512)),
        ],
        18,
        rows * channels * (2 * width + channels),
    )(meta, x_first, gain, scaled, cot, w_here, w_there, o_there)


def forward_kernel(meta, *refs, parts):
    received, refs = refs[: parts - 1], refs[parts - 1 :]
    (
        gain, qkv_in, w_here, w_there, o_here, o_there,
        update_out, qkv, raised_out, inverse_out, attended,
        o_full, scores_a, scores_b, peak_a, peak_b, low_a, low_b, values_t, outs_t, o_sems,
    ) = refs[:21]
    batch = meta[BATCH]
    half, width = w_here.shape
    channels = 2 * half
    rows = qkv.shape[0]
    count = update_out.shape[0]
    slot = pl.ds(aligned(meta[SLOT], HEAD_DIM), count)
    chunk = 512

    def o_copies():
        return weight_rows(o_here, o_there, o_full, o_sems)

    if parts > 1:
        w_full, scaled, w_sems = refs[21:]
        others = pl.ds(aligned(meta[OTHERS], HEAD_DIM), scaled.shape[0])
        extra = pl.ds(aligned(meta[EXTRA], HEAD_DIM), HEAD_DIM)
        chunks = width // chunk

        def weight_copies(index):
            at = span(index * chunk, chunk)
            return (
                pltpu.make_async_copy(w_here.at[:, at], w_full.at[pl.ds(0, half), at], w_sems.at[0, index]),
                pltpu.make_async_copy(w_there.at[:, at], w_full.at[pl.ds(half, half), at], w_sems.at[1, index]),
            )

        def start(index, carry):
            for copy in weight_copies(index):
                copy.start()
            return carry

        lax.fori_loop(0, chunks, start, 0)
        scale_rows(batch, received[0], gain, scaled)

        def project(index, carry):
            for copy in weight_copies(index):
                copy.wait()
            at = span(index * chunk, chunk)
            own = qkv[extra, at]
            qkv[others, at] = dot(scaled[...], w_full[:, at], 1, 0).astype(BF16)

            @pl.when(meta[ODD] == 1)
            def _():
                qkv[extra, at] = own

            return carry

        lax.fori_loop(0, chunks, project, 0)

    for copy in o_copies():
        copy.start()

    def columns(part, pair):
        return span(part * channels + pair * PAIR, PAIR)

    def scores(pair, head, out, peak):
        query = qkv[:, columns(0, pair)] * BF16(HEAD_DIM ** -0.5)
        values = dot(qkv[:, columns(1, pair)], head_mask(query, head), 1, 1)
        out[...] = values
        peak[...] = jnp.max(values, axis=0, keepdims=True)

    def softmax(head, source, peak, low):
        top = peak[...]
        sums = jnp.zeros((8, rows), F32)
        for at in range(0, rows, ROW_CHUNK):
            raised = jnp.exp(source[pl.ds(at, ROW_CHUNK), :] - top)
            raised_out[head, pl.ds(at, ROW_CHUNK), :] = raised
            sums = sums + jnp.sum(raised.reshape(ROW_CHUNK // 8, 8, rows), axis=0)
        inverse = 1.0 / jnp.sum(sums, axis=0, keepdims=True)
        inverse_out[head] = inverse
        for at in range(0, rows, ROW_CHUNK):
            low[pl.ds(at, ROW_CHUNK), :] = (raised_out[head, pl.ds(at, ROW_CHUNK), :] * inverse).astype(BF16)

    pairs = channels // PAIR
    scores(0, 0, scores_a, peak_a)

    def pair_of_heads(pair, carry):
        before = jnp.maximum(pair - 1, 0)
        after = jnp.minimum(pair + 1, pairs - 1)
        outs_t[HEAD_DIM:] = dot(values_t[HEAD_DIM:], low_b[...], 1, 0).astype(BF16)
        attended[:, columns(0, before)] = outs_t[...].T
        scores(pair, 1, scores_b, peak_b)
        softmax(2 * pair, scores_a, peak_a, low_a)
        values_t[...] = qkv[:, columns(2, pair)].T
        outs_t[:HEAD_DIM] = dot(values_t[:HEAD_DIM], low_a[...], 1, 0).astype(BF16)
        scores(after, 0, scores_a, peak_a)
        softmax(2 * pair + 1, scores_b, peak_b, low_b)
        return carry

    lax.fori_loop(0, pairs, pair_of_heads, 0, unroll=PAIRS_AT_ONCE)
    outs_t[HEAD_DIM:] = dot(values_t[HEAD_DIM:], low_b[...], 1, 0).astype(BF16)
    attended[:, columns(0, pairs - 1)] = outs_t[...].T
    for copy in o_copies():
        copy.wait()
    times_halves(batch, attended, slot, o_full, update_out, chunk)


def forward(meta, received, gain, qkv, w_here, w_there, o_here, o_there):
    rows, width = qkv.shape
    channels = width // 3
    count = sum(part.shape[0] for part in received)
    later = list(received[1:])
    heads = channels // HEAD_DIM
    return call(
        functools.partial(forward_kernel, parts=len(received)),
        "forward",
        [SCALAR] + [VECTOR] * (len(later) + 2) + [ANYWHERE] * 4,
        [VECTOR] * 5,
        [
            jax.ShapeDtypeStruct((count, channels), BF16),
            jax.ShapeDtypeStruct((rows, width), BF16),
            jax.ShapeDtypeStruct((heads, rows, rows), F32),
            jax.ShapeDtypeStruct((heads, 1, rows), F32),
            jax.ShapeDtypeStruct((rows, channels), BF16),
        ],
        [
            pltpu.VMEM((channels, channels), BF16),
            pltpu.VMEM((rows, rows), F32),
            pltpu.VMEM((rows, rows), F32),
            pltpu.VMEM((1, rows), F32),
            pltpu.VMEM((1, rows), F32),
            pltpu.VMEM((rows, rows), BF16),
            pltpu.VMEM((rows, rows), BF16),
            pltpu.VMEM((PAIR, rows), BF16),
            pltpu.VMEM((PAIR, rows), BF16),
            pltpu.SemaphoreType.DMA((2 * PIECES,)),
        ]
        + [
            pltpu.VMEM((channels, width), BF16),
            pltpu.VMEM((count - received[0].shape[0], channels), BF16),
            pltpu.SemaphoreType.DMA((2, width // 512)),
        ]
        * len(later),
        18,
        12 * 10 ** 9,
        aliases={len(later) + 2: 1},
    )(meta, *later, gain, qkv, w_here, w_there, o_here, o_there)


def backward_kernel(
    meta, x_first, x_others, c_slot, gain, qkv, raised, inverse, u_here, u_there, o_here, o_there, w_here, w_there,
    grad_out, grad_qkv,
    w_full, o_full, w_sems, o_sems, upstream, back, grads_a, grads_b, sum_a, sum_b, scores_a, scores_b, low_a, low_b, keys_t, dq_t, dk_sum, dv_sum,
):
    batch = meta[BATCH]
    count, channels = grad_out.shape
    half = channels // 2
    slot_start = meta[SLOT]
    slot = pl.ds(aligned(slot_start, HEAD_DIM), count)
    extra = pl.ds(aligned(meta[EXTRA], HEAD_DIM), HEAD_DIM)
    here, there = span(batch * half, half), span((1 - batch) * half, half)
    o_copies = weight_rows(o_here, o_there, o_full, o_sems)
    w_copies = weight_rows(w_here, w_there, w_full, w_sems)
    for copy in o_copies + w_copies:
        copy.start()
    upstream[:, here] = u_here[...]
    upstream[:, there] = u_there[...]
    for copy in o_copies:
        copy.wait()
    times_rows(batch, lambda: c_slot[...], o_full, upstream, slot, QUAD)

    @pl.when(meta[ODD] == 1)
    def _():
        upstream[extra, here] = u_here[extra, :]
        upstream[extra, there] = u_there[extra, :]

    def columns(part, pair):
        return span(part * channels + pair * PAIR, PAIR)

    def grad_probs(pair, head, out, row_sum):
        values = head_mask(qkv[:, columns(2, pair)], head)
        grads = dot(values, upstream[:, columns(0, pair)], 1, 1)
        out[...] = grads
        place = 2 * pair + head
        row_sum[...] = jnp.sum(grads * raised[place], axis=0, keepdims=True) * inverse[place]

    def score_grads(head, source, row_sum, scores, low):
        total = row_sum[...]
        scale = inverse[head]
        for at in range(0, source.shape[0], ROW_CHUNK):
            rows = pl.ds(at, ROW_CHUNK)
            soft = raised[head, rows, :] * scale
            low[rows, :] = soft.astype(BF16)
            scores[rows, :] = (soft * (source[rows, :] - total)).astype(BF16)

    def products(pair, head, scores, low):
        from_keys = dot(scores[...], head_mask(qkv[:, columns(0, pair)], head), 1, 0)
        from_values = dot(low[...], head_mask(upstream[:, columns(0, pair)], head), 1, 0)
        part = slice(HEAD_DIM * head, HEAD_DIM * head + HEAD_DIM)
        dq_t[part] = (dot(keys_t[part], scores[...], 1, 0) * HEAD_DIM ** -0.5).astype(BF16)
        if head == 0:
            dk_sum[...] = from_keys
            dv_sum[...] = from_values
        else:
            grad_qkv[:, columns(0, pair)] = dq_t[...].T
            grad_qkv[:, columns(1, pair)] = ((dk_sum[...] + from_keys) * HEAD_DIM ** -0.5).astype(BF16)
            grad_qkv[:, columns(2, pair)] = (dv_sum[...] + from_values).astype(BF16)

    pairs = channels // PAIR
    grad_probs(0, 0, grads_a, sum_a)

    def pair_of_heads(pair, carry):
        before = jnp.maximum(pair - 1, 0)
        after = jnp.minimum(pair + 1, pairs - 1)
        products(before, 1, scores_b, low_b)
        grad_probs(pair, 1, grads_b, sum_b)
        score_grads(2 * pair, grads_a, sum_a, scores_a, low_a)
        keys_t[...] = qkv[:, columns(1, pair)].T
        products(pair, 0, scores_a, low_a)
        grad_probs(after, 0, grads_a, sum_a)
        score_grads(2 * pair + 1, grads_b, sum_b, scores_b, low_b)
        return carry

    lax.fori_loop(0, pairs, pair_of_heads, 0, unroll=PAIRS_AT_ONCE)
    products(pairs - 1, 1, scores_b, low_b)
    for copy in w_copies:
        copy.wait()
    times_rows(batch, lambda: grad_qkv[slot, :], w_full, back, slice(None), QUAD)
    norm_backward_rows(x_first, back, gain, grad_out, meta[FIRST] - slot_start)
    if x_others is not None:
        norm_backward_rows(x_others, back, gain, grad_out, meta[OTHERS] - slot_start)


def backward(meta, x_parts, c_slot, gain, qkv, raised, inverse, u_here, u_there, o_here, o_there, w_here, w_there):
    rows, width = qkv.shape
    channels = width // 3
    count = c_slot.shape[0]

    def body(meta, *refs):
        if len(x_parts) == 1:
            backward_kernel(meta, refs[0], None, *refs[1:])
        else:
            backward_kernel(meta, *refs)

    square = (rows, rows)
    return call(
        body,
        "backward",
        [SCALAR] + [VECTOR] * (len(x_parts) + 7) + [ANYWHERE] * 4,
        [VECTOR] * 2,
        [jax.ShapeDtypeStruct((count, channels), BF16), jax.ShapeDtypeStruct((rows, width), BF16)],
        [
            pltpu.VMEM((channels, 3 * channels), BF16),
            pltpu.VMEM((channels, channels), BF16),
            pltpu.SemaphoreType.DMA((2 * PIECES,)),
            pltpu.SemaphoreType.DMA((2 * PIECES,)),
            pltpu.VMEM((rows, channels), BF16),
            pltpu.VMEM((count, channels), F32),
            pltpu.VMEM(square, F32),
            pltpu.VMEM(square, F32),
            pltpu.VMEM((1, rows), F32),
            pltpu.VMEM((1, rows), F32),
            pltpu.VMEM(square, BF16),
            pltpu.VMEM(square, BF16),
            pltpu.VMEM(square, BF16),
            pltpu.VMEM(square, BF16),
            pltpu.VMEM((PAIR, rows), BF16),
            pltpu.VMEM((PAIR, rows), BF16),
            pltpu.VMEM((rows, PAIR), F32),
            pltpu.VMEM((rows, PAIR), F32),
        ],
        18,
        20 * 10 ** 9,
    )(meta, *x_parts, c_slot, gain, qkv, raised, inverse, u_here, u_there, o_here, o_there, w_here, w_there)


def finish_kernel(
    meta, tokens, gain, attended, grad_qkv, received, o_here, o_there, w_here, w_there,
    update, grad,
    w_full, o_full, w_sems, o_sems, back,
):
    batch = meta[BATCH]
    rows, channels = tokens.shape
    count = received.shape[0]
    everything = slice(None)
    o_copies = weight_rows(o_here, o_there, o_full, o_sems)
    w_copies = weight_rows(w_here, w_there, w_full, w_sems)
    for copy in o_copies + w_copies:
        copy.start()
    for copy in o_copies:
        copy.wait()
    times_halves(batch, attended, everything, o_full, update, QUAD)
    extra = pl.ds(aligned(meta[EXTRA], HEAD_DIM), HEAD_DIM)
    kept = update[extra, :]
    update[pl.ds(aligned(meta[SLOT], HEAD_DIM), count), :] = received[...]

    @pl.when(meta[ODD] == 1)
    def _():
        update[extra, :] = kept

    for copy in w_copies:
        copy.wait()
    times_rows(batch, lambda: grad_qkv[...], w_full, back, everything, QUAD)
    norm_backward_rows(tokens, back, gain, grad)


def finish(meta, tokens, gain, attended, grad_qkv, received, o_here, o_there, w_here, w_there):
    rows, channels = tokens.shape
    block = jax.ShapeDtypeStruct((rows, channels), BF16)
    return call(
        finish_kernel,
        "finish",
        [SCALAR] + [VECTOR] * 5 + [ANYWHERE] * 4,
        [VECTOR] * 2,
        [block] * 2,
        [
            pltpu.VMEM((channels, 3 * channels), BF16),
            pltpu.VMEM((channels, channels), BF16),
            pltpu.SemaphoreType.DMA((2 * PIECES,)),
            pltpu.SemaphoreType.DMA((2 * PIECES,)),
            pltpu.VMEM((rows, channels), F32),
        ],
        18,
        8 * rows * channels * channels,
    )(meta, tokens, gain, attended, grad_qkv, received, o_here, o_there, w_here, w_there)


def merge_kernel(meta, grad_back, grad, out, sems):
    count = grad_back.shape[0]
    extra = meta[EXTRA] - meta[SLOT]

    def row_copy(index, source, at):
        place = pl.ds(aligned(meta[SLOT] + index * HEAD_DIM, HEAD_DIM), HEAD_DIM)
        return pltpu.make_async_copy(source.at[at], out.at[place], sems.at[index])

    def kept_copy(index):
        place = span(lax.rem(meta[SLOT] + count, grad.shape[0]) + index * HEAD_DIM, HEAD_DIM)
        return pltpu.make_async_copy(grad.at[place], out.at[place], sems.at[count // HEAD_DIM + index])

    kept = (grad.shape[0] - count) // HEAD_DIM
    for index in range(kept):
        kept_copy(index).start()
    for index in range(count // HEAD_DIM):
        own = (meta[ODD] == 1) & (extra == index * HEAD_DIM)
        place = pl.ds(aligned(meta[SLOT] + index * HEAD_DIM, HEAD_DIM), HEAD_DIM)

        @pl.when(own)
        def _(index=index, place=place):
            row_copy(index, grad, place).start()

        @pl.when(jnp.logical_not(own))
        def _(index=index):
            row_copy(index, grad_back, pl.ds(index * HEAD_DIM, HEAD_DIM)).start()

    for index in range(kept):
        kept_copy(index).wait()
    for index in range(count // HEAD_DIM):
        row_copy(index, grad_back, pl.ds(index * HEAD_DIM, HEAD_DIM)).wait()


def merge(meta, grad_back, grad):
    return call(
        merge_kernel, "merge", [SCALAR] + [VECTOR] * 2, pl.BlockSpec(memory_space=pltpu.HBM),
        jax.ShapeDtypeStruct(grad.shape, BF16), [pltpu.SemaphoreType.DMA((grad.shape[0] // HEAD_DIM,))], 4, 0,
    )(meta, grad_back, grad)


def after_kernel(rows, earlier, out):
    pass


def after(rows, earlier):
    return call(
        after_kernel, "after", [ANYWHERE] * 2, ANYWHERE, jax.ShapeDtypeStruct(rows.shape, BF16), [], 18, 0,
        aliases={0: 0},
    )(rows, earlier)


def exchange(rows, near, back):
    size = lax.axis_size("space")

    def along(by):
        return lax.ppermute(rows, "space", [(i, (i + by) % size) for i in range(size)])

    if size == 2 * YTILES:
        return along(YTILES)
    return jnp.where(near != back, along(-YTILES), along(YTILES))


def swapped(part):
    return lax.ppermute(part, "batch", [(0, 1), (1, 0)])


def shards(inputs, cotangent, offsets, w_qkv, w_out, gain):
    tiled_shape = inputs.shape
    channels = tiled_shape[-1]
    row = WIN * tiled_shape[4]
    tokens = inputs.reshape(-1, channels)
    cot = cotangent.reshape(-1, channels)
    gain = gain.reshape(1, channels)
    shift = offsets[0]
    near = shift <= HALF_WIN
    moved = jnp.minimum(shift, WIN - shift)
    batch = lax.axis_index("batch")

    first = jnp.where(near, 0, (WIN - LEAD) * row)
    o_there = swapped(w_out)
    w_there = swapped(w_qkv)
    x_first = exchange(lax.dynamic_slice_in_dim(tokens, first, LEAD * row, 0), near, False)

    def meta_of(count):
        slot = jnp.where(near, 0, (WIN - count) * row)
        others = jnp.where(near, LEAD * row, (WIN - count) * row)
        extra = jnp.where(near, (count - 1) * row, (WIN - count) * row)
        return jnp.stack([batch, slot, first, others, extra, moved % 2]).astype(jnp.int32)

    scaled, u_here, x_sent, c_sent, c_sent_few = own_tokens(meta_of(LEAD), tokens, cot, gain, w_out)

    def branch(count):
        def run(tokens, cot, x_first, x_sent, c_sent, c_sent_few, scaled, u_here, w_qkv, w_there, w_out, o_there):
            meta = meta_of(count)
            if count > LEAD:
                received = (x_first, exchange(x_sent, near, False))
                c_slot = exchange(after(c_sent, received[1]), near, False)
            else:
                received = (x_first,)
                c_slot = exchange(c_sent_few, near, False)
            qkv, u_there = rest_projection(meta, x_first, gain, scaled, cot, w_qkv, w_there, o_there)
            weights = (w_out, o_there, w_qkv, w_there)
            update_sent, window, raised, inverse, attended = forward(
                meta, received, gain, qkv, w_qkv, w_there, w_out, o_there
            )
            update_back = exchange(after(update_sent, c_slot), near, True)
            grad_sent, grad_qkv = backward(
                meta, received, c_slot, gain, window, raised, inverse, u_here, u_there, *weights
            )
            grad_back = exchange(grad_sent, near, True)
            update, grad = finish(meta, tokens, gain, attended, grad_qkv, update_back, *weights)
            return update, merge(meta, grad_back, grad)

        return run

    update, grad = lax.cond(
        moved <= LEAD, branch(LEAD), branch(HALF_WIN),
        tokens, cot, x_first, x_sent, c_sent, c_sent_few, scaled, u_here, w_qkv, w_there, w_out, o_there,
    )
    return (update.reshape(tiled_shape), grad.reshape(tiled_shape))


def solution(mesh):
    in_specs = (
        P(("groups", "batch"), "space", None, None, None, None),
        P(("groups", "batch"), "space", None, None, None, None),
        P(("groups", "batch")),
        P("batch", None),
        P("batch", None),
        P(),
    )
    out_specs = (
        P(("groups", "batch"), "space", None, None, None, None),
        P(("groups", "batch"), "space", None, None, None, None),
    )
    return jax.shard_map(shards, mesh=mesh, in_specs=in_specs, out_specs=out_specs, check_vma=False)
```

```python
import functools

import jax
import jax.numpy as jnp
from jax import lax
from jax.experimental import pallas as pl
from jax.experimental.pallas import tpu as pltpu
from jax.sharding import PartitionSpec as P

WIN = 8
YTILES = 4
HEAD_DIM = 64
EPS = 1e-05
PAIR = 2 * HEAD_DIM
QUAD = 4 * HEAD_DIM
HALF_WIN = WIN // 2
LEAD = 1
COUNTS = (2, 3, 4)
BF16 = jnp.bfloat16
F32 = jnp.float32
NORM_ROWS = 64
ROW_CHUNK = 64
PIECES = 4
KERNEL_MIB = 12
ANYWHERE = pl.BlockSpec(memory_space=pltpu.HBM)
VECTOR = pl.BlockSpec(memory_space=pltpu.VMEM)
SCALAR = pl.BlockSpec(memory_space=pltpu.SMEM)
NORM_ROWS = 64
ROW_CHUNK = 64
PIECES = 4
KERNEL_MIB = 12
PAIRS_AT_ONCE = 1


def dot(left, right, left_dim, right_dim):
    return lax.dot_general(
        left, right, (((left_dim,), (right_dim,)), ((), ())), preferred_element_type=F32
    )


def normalise(tokens):
    values32 = tokens.astype(F32)
    center = values32 - jnp.mean(values32, axis=-1, keepdims=True)
    inverse = lax.rsqrt(jnp.mean(center * center, axis=-1, keepdims=True) + EPS)
    return center * inverse, inverse


def norm_backward(tokens, grad_scaled, gain):
    normed, inverse = normalise(tokens)
    grad_normed = grad_scaled * gain
    mean_grad = jnp.mean(grad_normed, axis=-1, keepdims=True)
    mean_mixed = jnp.mean(grad_normed * normed, axis=-1, keepdims=True)
    return (inverse * (grad_normed - mean_grad - normed * mean_mixed)).astype(BF16)


def head_mask(pair, head):
    lane = lax.broadcasted_iota(jnp.int32, pair.shape, 1)
    return jnp.where((lane < HEAD_DIM) == (head == 0), pair, jnp.zeros_like(pair))


def aligned(value, multiple):
    return pl.multiple_of(value, multiple)


def span(start, size):
    return pl.ds(aligned(start, size), size)


def call(kernel, name, in_specs, out_specs, out_shape, scratch, flops, aliases=None):
    return pl.pallas_call(
        kernel,
        in_specs=in_specs,
        out_specs=out_specs,
        out_shape=out_shape,
        scratch_shapes=scratch,
        compiler_params=pltpu.CompilerParams(vmem_limit_bytes=KERNEL_MIB << 20),
        cost_estimate=pl.CostEstimate(flops=flops, bytes_accessed=1 << 20, transcendentals=0),
        input_output_aliases=aliases or {},
        name=name,
    )


BATCH, SLOT, FIRST, OTHERS, EXTRA, ODD = range(6)


def over_rows(count, body):
    def step(index, carry):
        body(span(index * NORM_ROWS, NORM_ROWS))
        return carry

    lax.fori_loop(0, count // NORM_ROWS, step, 0)


def shifted(rows, by):
    return pl.ds(aligned(rows.start + by, HEAD_DIM), rows.size)


def scale_rows(batch, tokens, gain, scaled, into=0):
    half = tokens.shape[1] // 2

    def body(rows):
        normed, _ = normalise(tokens[rows, :])
        values = (normed * gain[...]).astype(BF16)
        place = shifted(rows, into)
        scaled[place, :half] = jnp.where(batch == 0, values[:, :half], values[:, half:])
        scaled[place, half:] = jnp.where(batch == 0, values[:, half:], values[:, :half])

    over_rows(tokens.shape[0], body)


def norm_backward_rows(tokens, back, gain, out, at=0):
    def body(rows):
        place = shifted(rows, at)
        out[place, :] = norm_backward(tokens[rows, :], back[place, :], gain[...])

    over_rows(tokens.shape[0], body)


def times_rows(batch, left, weights, out, rows, chunk):
    half = weights.shape[0] // 2
    per_half = half // chunk

    def columns(index, carry):
        place = jnp.where(index < per_half, batch, 1 - batch) * half + lax.rem(index, per_half) * chunk
        product = dot(left(), weights[span(index * chunk, chunk), :], 1, 1)
        out[rows, span(place, chunk)] = product.astype(out.dtype)
        return carry

    lax.fori_loop(0, 2 * per_half, columns, 0)


def times_halves(batch, left, rows, weights, out, chunk):
    half = weights.shape[0] // 2

    def columns(index, carry):
        at = span(index * chunk, chunk)
        product = dot(left[rows, span(batch * half, half)], weights[:half, at], 1, 0)
        product = product + dot(left[rows, span((1 - batch) * half, half)], weights[half:, at], 1, 0)
        out[:, at] = product.astype(BF16)
        return carry

    lax.fori_loop(0, weights.shape[1] // chunk, columns, 0)


def weight_rows(here, there, full, sems):
    half = here.shape[0]
    size = half // PIECES
    return tuple(
        pltpu.make_async_copy(
            source.at[pl.ds(piece * size, size)],
            full.at[pl.ds(place * half + piece * size, size)],
            sems.at[place * PIECES + piece],
        )
        for place, source in enumerate((here, there))
        for piece in range(PIECES)
    )


def multiply_columns(tokens, weights, out):
    def columns(index, carry):
        at = span(index * QUAD, QUAD)
        out[:, at] = dot(tokens[...], weights[at, :], 1, 1).astype(BF16)
        return carry

    lax.fori_loop(0, weights.shape[0] // QUAD, columns, 0)


def own_kernel(meta, tokens, cot, gain, o_here, scaled, upstream, *sent):
    scale_rows(meta[BATCH], tokens, gain, scaled)
    multiply_columns(cot, o_here, upstream)
    near = meta[SLOT] == 0

    def cut(source, out, if_near, if_far):
        start = aligned(jnp.where(near, if_near, if_far) * HEAD_DIM, HEAD_DIM)
        out[...] = source[pl.ds(start, out.shape[0]), :]

    for index, count in enumerate(COUNTS):
        cut(tokens, sent[2 * index], LEAD, WIN - count)
        cut(cot, sent[2 * index + 1], 0, WIN - count)


def own_tokens(meta, tokens, cot, gain, o_here):
    rows, channels = tokens.shape
    half = o_here.shape[0]
    shapes = [(rows, channels), (rows, half)]
    for count in COUNTS:
        shapes += [((count - LEAD) * HEAD_DIM, channels), (count * HEAD_DIM, channels)]
    return call(
        own_kernel,
        "own_tokens",
        [SCALAR] + [VECTOR] * 4,
        [VECTOR] * len(shapes),
        [jax.ShapeDtypeStruct(shape, BF16) for shape in shapes],
        [],
        rows * channels * channels,
    )(meta, tokens, cot, gain, o_here)


def rest_kernel(
    meta, x_first, gain, scaled_in, cot_in, w_here, w_there, o_here, o_there, qkv, upstream, w_full, o_full,
    scaled, cot, sems, w_sems, o_sems,
):
    half, width = w_here.shape
    rows = qkv.shape[0]
    first = pl.ds(aligned(meta[FIRST], HEAD_DIM), x_first.shape[0])
    chunk = 512
    chunks = width // chunk
    scaled_copy = pltpu.make_async_copy(scaled_in, scaled.at[pl.ds(0, rows)], sems.at[0])
    later = (pltpu.make_async_copy(cot_in, cot, sems.at[1]),) + weight_rows(o_here, o_there, o_full, o_sems)

    def weight_copies(index):
        at = pl.ds(aligned(index * chunk, chunk), chunk)
        return (
            pltpu.make_async_copy(w_here.at[:, at], w_full.at[pl.ds(0, half), at], w_sems.at[0, index]),
            pltpu.make_async_copy(w_there.at[:, at], w_full.at[pl.ds(half, half), at], w_sems.at[1, index]),
        )

    scaled_copy.start()

    def start_weights(index, carry):
        for copy in weight_copies(index):
            copy.start()
        return carry

    lax.fori_loop(0, chunks, start_weights, 0)
    for copy in later:
        copy.start()
    scale_rows(meta[BATCH], x_first, gain, scaled, rows)
    scaled_copy.wait()

    def project(index, carry):
        for copy in weight_copies(index):
            copy.wait()
        at = pl.ds(aligned(index * chunk, chunk), chunk)
        product = dot(scaled[...], w_full[:, at], 1, 0).astype(BF16)
        qkv[:, at] = product[:rows]
        qkv[first, at] = product[rows:]
        return carry

    lax.fori_loop(0, chunks, project, 0)
    for copy in later:
        copy.wait()
    multiply_columns(cot, o_full.at[pl.ds(half, half)], upstream)


def rest_projection(meta, x_first, gain, scaled, cot, w_here, w_there, o_here, o_there):
    rows, channels = scaled.shape
    half, width = w_there.shape
    shapes = [(rows, width), (rows, half), (channels, width), (channels, channels)]
    return call(
        rest_kernel,
        "rest_projection",
        [SCALAR] + [VECTOR] * 2 + [ANYWHERE] * 6,
        [VECTOR] * 4,
        [jax.ShapeDtypeStruct(shape, BF16) for shape in shapes],
        [
            pltpu.VMEM((rows + x_first.shape[0], channels), BF16),
            pltpu.VMEM((rows, channels), BF16),
            pltpu.SemaphoreType.DMA((2,)),
            pltpu.SemaphoreType.DMA((2, width // 512)),
            pltpu.SemaphoreType.DMA((2 * PIECES,)),
        ],
        rows * channels * (2 * width + channels),
    )(meta, x_first, gain, scaled, cot, w_here, w_there, o_here, o_there)


def forward_kernel(
    meta, x_others, gain, qkv_in, w_full, o_full,
    update_out, qkv, raised_out, inverse_out, attended,
    scaled, scores_a, scores_b, peak_a, peak_b, low_a, low_b, values_t, outs_t,
):
    batch = meta[BATCH]
    channels, width = w_full.shape
    rows = qkv.shape[0]
    count = update_out.shape[0]
    slot = pl.ds(aligned(meta[SLOT], HEAD_DIM), count)
    others = pl.ds(aligned(meta[OTHERS], HEAD_DIM), scaled.shape[0])
    extra = pl.ds(aligned(meta[EXTRA], HEAD_DIM), HEAD_DIM)
    chunk = 512
    scale_rows(batch, x_others, gain, scaled)

    def project(index, carry):
        at = span(index * chunk, chunk)
        own = qkv[extra, at]
        qkv[others, at] = dot(scaled[...], w_full[:, at], 1, 0).astype(BF16)

        @pl.when(meta[ODD] == 1)
        def _():
            qkv[extra, at] = own

        return carry

    lax.fori_loop(0, width // chunk, project, 0)

    def columns(part, pair):
        return span(part * channels + pair * PAIR, PAIR)

    def scores(pair, head, out, peak):
        query = qkv[:, columns(0, pair)] * BF16(HEAD_DIM ** -0.5)
        values = dot(qkv[:, columns(1, pair)], head_mask(query, head), 1, 1)
        out[...] = values
        peak[...] = jnp.max(values, axis=0, keepdims=True)

    def softmax(head, source, peak, low):
        top = peak[...]
        sums = jnp.zeros((8, rows), F32)
        for at in range(0, rows, ROW_CHUNK):
            raised = jnp.exp(source[pl.ds(at, ROW_CHUNK), :] - top)
            raised_out[head, pl.ds(at, ROW_CHUNK), :] = raised
            sums = sums + jnp.sum(raised.reshape(ROW_CHUNK // 8, 8, rows), axis=0)
        inverse = 1.0 / jnp.sum(sums, axis=0, keepdims=True)
        inverse_out[head] = inverse
        for at in range(0, rows, ROW_CHUNK):
            low[pl.ds(at, ROW_CHUNK), :] = (raised_out[head, pl.ds(at, ROW_CHUNK), :] * inverse).astype(BF16)

    pairs = channels // PAIR
    scores(0, 0, scores_a, peak_a)

    def pair_of_heads(pair, carry):
        before = jnp.maximum(pair - 1, 0)
        after = jnp.minimum(pair + 1, pairs - 1)
        outs_t[HEAD_DIM:] = dot(values_t[HEAD_DIM:], low_b[...], 1, 0).astype(BF16)
        attended[:, columns(0, before)] = outs_t[...].T
        scores(pair, 1, scores_b, peak_b)
        softmax(2 * pair, scores_a, peak_a, low_a)
        values_t[...] = qkv[:, columns(2, pair)].T
        outs_t[:HEAD_DIM] = dot(values_t[:HEAD_DIM], low_a[...], 1, 0).astype(BF16)
        scores(after, 0, scores_a, peak_a)
        softmax(2 * pair + 1, scores_b, peak_b, low_b)
        return carry

    lax.fori_loop(0, pairs, pair_of_heads, 0, unroll=PAIRS_AT_ONCE)
    outs_t[HEAD_DIM:] = dot(values_t[HEAD_DIM:], low_b[...], 1, 0).astype(BF16)
    attended[:, columns(0, pairs - 1)] = outs_t[...].T
    times_halves(batch, attended, slot, o_full, update_out, chunk)


def forward(meta, x_others, gain, qkv, w_full, o_full):
    rows, width = qkv.shape
    channels = width // 3
    count = x_others.shape[0] + LEAD * HEAD_DIM
    heads = channels // HEAD_DIM
    return call(
        forward_kernel,
        "forward",
        [SCALAR] + [VECTOR] * 5,
        [VECTOR] * 5,
        [
            jax.ShapeDtypeStruct((count, channels), BF16),
            jax.ShapeDtypeStruct((rows, width), BF16),
            jax.ShapeDtypeStruct((heads, rows, rows), F32),
            jax.ShapeDtypeStruct((heads, 1, rows), F32),
            jax.ShapeDtypeStruct((rows, channels), BF16),
        ],
        [
            pltpu.VMEM(x_others.shape, BF16),
            pltpu.VMEM((rows, rows), F32),
            pltpu.VMEM((rows, rows), F32),
            pltpu.VMEM((1, rows), F32),
            pltpu.VMEM((1, rows), F32),
            pltpu.VMEM((rows, rows), BF16),
            pltpu.VMEM((rows, rows), BF16),
            pltpu.VMEM((PAIR, rows), BF16),
            pltpu.VMEM((PAIR, rows), BF16),
        ],
        12 * 10 ** 9,
        aliases={3: 1},
    )(meta, x_others, gain, qkv, w_full, o_full)


def backward_kernel(
    meta, x_first, x_others, c_slot, gain, qkv, raised, inverse, u_here, u_there, w_full, o_full,
    grad_out, grad_qkv,
    upstream, back, grads_a, grads_b, sum_a, sum_b, scores_a, scores_b, low_a, low_b, keys_t, dq_t, dk_sum, dv_sum,
):
    batch = meta[BATCH]
    count, channels = grad_out.shape
    half = channels // 2
    slot_start = meta[SLOT]
    slot = pl.ds(aligned(slot_start, HEAD_DIM), count)
    extra = pl.ds(aligned(meta[EXTRA], HEAD_DIM), HEAD_DIM)
    here, there = span(batch * half, half), span((1 - batch) * half, half)
    upstream[:, here] = u_here[...]
    upstream[:, there] = u_there[...]
    times_rows(batch, lambda: c_slot[...], o_full, upstream, slot, QUAD)

    @pl.when(meta[ODD] == 1)
    def _():
        upstream[extra, here] = u_here[extra, :]
        upstream[extra, there] = u_there[extra, :]

    def columns(part, pair):
        return span(part * channels + pair * PAIR, PAIR)

    def grad_probs(pair, head, out, row_sum):
        values = head_mask(qkv[:, columns(2, pair)], head)
        grads = dot(values, upstream[:, columns(0, pair)], 1, 1)
        out[...] = grads
        place = 2 * pair + head
        row_sum[...] = jnp.sum(grads * raised[place], axis=0, keepdims=True) * inverse[place]

    def score_grads(head, source, row_sum, scores, low):
        total = row_sum[...]
        scale = inverse[head]
        for at in range(0, source.shape[0], ROW_CHUNK):
            rows = pl.ds(at, ROW_CHUNK)
            soft = raised[head, rows, :] * scale
            low[rows, :] = soft.astype(BF16)
            scores[rows, :] = (soft * (source[rows, :] - total)).astype(BF16)

    def products(pair, head, scores, low):
        from_keys = dot(scores[...], head_mask(qkv[:, columns(0, pair)], head), 1, 0)
        from_values = dot(low[...], head_mask(upstream[:, columns(0, pair)], head), 1, 0)
        part = slice(HEAD_DIM * head, HEAD_DIM * head + HEAD_DIM)
        dq_t[part] = (dot(keys_t[part], scores[...], 1, 0) * HEAD_DIM ** -0.5).astype(BF16)
        if head == 0:
            dk_sum[...] = from_keys
            dv_sum[...] = from_values
        else:
            grad_qkv[:, columns(0, pair)] = dq_t[...].T
            grad_qkv[:, columns(1, pair)] = ((dk_sum[...] + from_keys) * HEAD_DIM ** -0.5).astype(BF16)
            grad_qkv[:, columns(2, pair)] = (dv_sum[...] + from_values).astype(BF16)

    pairs = channels // PAIR
    grad_probs(0, 0, grads_a, sum_a)

    def pair_of_heads(pair, carry):
        before = jnp.maximum(pair - 1, 0)
        after = jnp.minimum(pair + 1, pairs - 1)
        products(before, 1, scores_b, low_b)
        grad_probs(pair, 1, grads_b, sum_b)
        score_grads(2 * pair, grads_a, sum_a, scores_a, low_a)
        keys_t[...] = qkv[:, columns(1, pair)].T
        products(pair, 0, scores_a, low_a)
        grad_probs(after, 0, grads_a, sum_a)
        score_grads(2 * pair + 1, grads_b, sum_b, scores_b, low_b)
        return carry

    lax.fori_loop(0, pairs, pair_of_heads, 0, unroll=PAIRS_AT_ONCE)
    products(pairs - 1, 1, scores_b, low_b)
    times_rows(batch, lambda: grad_qkv[slot, :], w_full, back, slice(None), QUAD)
    norm_backward_rows(x_first, back, gain, grad_out, meta[FIRST] - slot_start)
    norm_backward_rows(x_others, back, gain, grad_out, meta[OTHERS] - slot_start)


def backward(meta, x_first, x_others, c_slot, gain, qkv, raised, inverse, u_here, u_there, w_full, o_full):
    rows, width = qkv.shape
    channels = width // 3
    count = c_slot.shape[0]
    square = (rows, rows)
    return call(
        backward_kernel,
        "backward",
        [SCALAR] + [VECTOR] * 11,
        [VECTOR] * 2,
        [jax.ShapeDtypeStruct((count, channels), BF16), jax.ShapeDtypeStruct((rows, width), BF16)],
        [
            pltpu.VMEM((rows, channels), BF16),
            pltpu.VMEM((count, channels), F32),
            pltpu.VMEM(square, F32),
            pltpu.VMEM(square, F32),
            pltpu.VMEM((1, rows), F32),
            pltpu.VMEM((1, rows), F32),
            pltpu.VMEM(square, BF16),
            pltpu.VMEM(square, BF16),
            pltpu.VMEM(square, BF16),
            pltpu.VMEM(square, BF16),
            pltpu.VMEM((PAIR, rows), BF16),
            pltpu.VMEM((PAIR, rows), BF16),
            pltpu.VMEM((rows, PAIR), F32),
            pltpu.VMEM((rows, PAIR), F32),
        ],
        20 * 10 ** 9,
    )(meta, x_first, x_others, c_slot, gain, qkv, raised, inverse, u_here, u_there, w_full, o_full)


def finish_kernel(
    meta, tokens, gain, attended, grad_qkv, received, w_full, o_full, update_out, grad_out,
    update, grad, back, sems,
):
    batch = meta[BATCH]
    rows, channels = tokens.shape
    count = received.shape[0]
    everything = slice(None)

    def copies(source, out, which):
        size = rows // PIECES
        return tuple(
            pltpu.make_async_copy(
                source.at[pl.ds(piece * size, size)], out.at[pl.ds(piece * size, size)], sems.at[which, piece]
            )
            for piece in range(PIECES)
        )

    times_halves(batch, attended, everything, o_full, update, QUAD)
    extra = pl.ds(aligned(meta[EXTRA], HEAD_DIM), HEAD_DIM)
    kept = update[extra, :]
    update[pl.ds(aligned(meta[SLOT], HEAD_DIM), count), :] = received[...]

    @pl.when(meta[ODD] == 1)
    def _():
        update[extra, :] = kept

    for copy in copies(update, update_out, 0):
        copy.start()
    times_rows(batch, lambda: grad_qkv[...], w_full, back, everything, QUAD)
    norm_backward_rows(tokens, back, gain, grad)
    for copy in copies(grad, grad_out, 1):
        copy.start()
    for copy in copies(update, update_out, 0) + copies(grad, grad_out, 1):
        copy.wait()


def finish(meta, tokens, gain, attended, grad_qkv, received, w_full, o_full):
    rows, channels = tokens.shape
    block = jax.ShapeDtypeStruct((rows, channels), BF16)
    return call(
        finish_kernel,
        "finish",
        [SCALAR] + [VECTOR] * 7,
        [ANYWHERE] * 2,
        [block] * 2,
        [
            pltpu.VMEM((rows, channels), BF16),
            pltpu.VMEM((rows, channels), BF16),
            pltpu.VMEM((rows, channels), F32),
            pltpu.SemaphoreType.DMA((2, PIECES)),
        ],
        8 * rows * channels * channels,
    )(meta, tokens, gain, attended, grad_qkv, received, w_full, o_full)


def merge_kernel(meta, grad_back, grad, out, sems):
    for index in range(grad_back.shape[0] // HEAD_DIM):
        start = aligned(meta[SLOT] + index * HEAD_DIM, HEAD_DIM)
        copy = pltpu.make_async_copy(
            grad_back.at[pl.ds(index * HEAD_DIM, HEAD_DIM)], out.at[pl.ds(start, HEAD_DIM)], sems.at[index]
        )
        wanted = jnp.logical_not((meta[ODD] == 1) & (start == meta[EXTRA]))
        pl.when(wanted)(copy.start)

    for index in range(grad_back.shape[0] // HEAD_DIM):
        start = aligned(meta[SLOT] + index * HEAD_DIM, HEAD_DIM)
        copy = pltpu.make_async_copy(
            grad_back.at[pl.ds(index * HEAD_DIM, HEAD_DIM)], out.at[pl.ds(start, HEAD_DIM)], sems.at[index]
        )
        wanted = jnp.logical_not((meta[ODD] == 1) & (start == meta[EXTRA]))
        pl.when(wanted)(copy.wait)


def merge(meta, grad_back, grad):
    return call(
        merge_kernel, "merge", [SCALAR, VECTOR, ANYWHERE], ANYWHERE, jax.ShapeDtypeStruct(grad.shape, BF16),
        [pltpu.SemaphoreType.DMA((HALF_WIN,))], 0, aliases={2: 0},
    )(meta, grad_back, grad)


def after_kernel(rows, earlier, out):
    pass


def after(rows, earlier):
    return call(
        after_kernel, "after", [ANYWHERE] * 2, ANYWHERE, jax.ShapeDtypeStruct(rows.shape, BF16), [], 0,
        aliases={0: 0},
    )(rows, earlier)


def exchange(rows, near, back):
    size = lax.axis_size("space")

    def along(by):
        return lax.ppermute(rows, "space", [(i, (i + by) % size) for i in range(size)])

    if size == 2 * YTILES:
        return along(YTILES)
    return jnp.where(near != back, along(-YTILES), along(YTILES))


def swapped(part):
    return lax.ppermute(part, "batch", [(0, 1), (1, 0)])


def shards(inputs, cotangent, offsets, w_qkv, w_out, gain):
    tiled_shape = inputs.shape
    channels = tiled_shape[-1]
    row = WIN * tiled_shape[4]
    tokens = inputs.reshape(-1, channels)
    cot = cotangent.reshape(-1, channels)
    gain = gain.reshape(1, channels)
    shift = offsets[0]
    near = shift <= HALF_WIN
    moved = jnp.minimum(shift, WIN - shift)
    batch = lax.axis_index("batch")

    first = jnp.where(near, 0, (WIN - LEAD) * row)
    o_there = swapped(w_out)
    w_there = swapped(w_qkv)
    x_first = exchange(lax.dynamic_slice_in_dim(tokens, first, LEAD * row, 0), near, False)

    def meta_of(count):
        slot = jnp.where(near, 0, (WIN - count) * row)
        others = jnp.where(near, LEAD * row, (WIN - count) * row)
        extra = jnp.where(near, (count - 1) * row, (WIN - count) * row)
        return jnp.stack([batch, slot, first, others, extra, moved < count]).astype(jnp.int32)

    scaled, u_here, *sent = own_tokens(meta_of(COUNTS[0]), tokens, cot, gain, w_out)

    def branch(count):
        def run(tokens, cot, x_first, scaled, u_here, weights, sent):
            meta = meta_of(count)
            x_sent, c_sent = sent[2 * COUNTS.index(count) :][:2]
            x_others = exchange(x_sent, near, False)
            c_slot = exchange(after(c_sent, x_others), near, False)
            qkv, u_there, w_full, o_full = rest_projection(meta, x_first, gain, scaled, cot, *weights)
            update_sent, window, raised, inverse, attended = forward(meta, x_others, gain, qkv, w_full, o_full)
            update_back = exchange(after(update_sent, c_slot), near, True)
            grad_sent, grad_qkv = backward(
                meta, x_first, x_others, c_slot, gain, window, raised, inverse, u_here, u_there, w_full, o_full
            )
            grad_back = exchange(grad_sent, near, True)
            update, grad = finish(meta, tokens, gain, attended, grad_qkv, update_back, w_full, o_full)
            return update, merge(meta, grad_back, grad)

        return run

    update, grad = lax.switch(
        jnp.maximum(moved, COUNTS[0]) - COUNTS[0],
        [branch(count) for count in COUNTS],
        tokens, cot, x_first, scaled, u_here, (w_qkv, w_there, w_out, o_there), tuple(sent),
    )
    return (update.reshape(tiled_shape), grad.reshape(tiled_shape))


def solution(mesh):
    in_specs = (
        P(("groups", "batch"), "space", None, None, None, None),
        P(("groups", "batch"), "space", None, None, None, None),
        P(("groups", "batch")),
        P("batch", None),
        P("batch", None),
        P(),
    )
    out_specs = (
        P(("groups", "batch"), "space", None, None, None, None),
        P(("groups", "batch"), "space", None, None, None, None),
    )
    return jax.shard_map(shards, mesh=mesh, in_specs=in_specs, out_specs=out_specs, check_vma=False)
```

```python
import functools

import jax
import jax.numpy as jnp
from jax import lax
from jax.experimental import pallas as pl
from jax.experimental.pallas import tpu as pltpu
from jax.sharding import PartitionSpec as P

WIN = 8
YTILES = 4
HEAD_DIM = 64
EPS = 1e-05
PAIR = 2 * HEAD_DIM
QUAD = 4 * HEAD_DIM
HALF_WIN = WIN // 2
LEAD = 1
COUNTS = (2, 3, 4)
HALVED = ()
BF16 = jnp.bfloat16
F32 = jnp.float32
NORM_ROWS = 64
ROW_CHUNK = 64
FEW_ROWS = 16
PIECES = 4
KERNEL_MIB = 12
ANYWHERE = pl.BlockSpec(memory_space=pltpu.HBM)
VECTOR = pl.BlockSpec(memory_space=pltpu.VMEM)
SCALAR = pl.BlockSpec(memory_space=pltpu.SMEM)
NORM_ROWS = 64
ROW_CHUNK = 64
FEW_ROWS = 16
PIECES = 4
KERNEL_MIB = 12
PAIRS_AT_ONCE = 2


def dot(left, right, left_dim, right_dim):
    return lax.dot_general(
        left, right, (((left_dim,), (right_dim,)), ((), ())), preferred_element_type=F32
    )


def normalise(tokens):
    values32 = tokens.astype(F32)
    center = values32 - jnp.mean(values32, axis=-1, keepdims=True)
    inverse = lax.rsqrt(jnp.mean(center * center, axis=-1, keepdims=True) + EPS)
    return center * inverse, inverse


def norm_backward(tokens, grad_scaled, gain):
    normed, inverse = normalise(tokens)
    grad_normed = grad_scaled * gain
    mean_grad = jnp.mean(grad_normed, axis=-1, keepdims=True)
    mean_mixed = jnp.mean(grad_normed * normed, axis=-1, keepdims=True)
    return (inverse * (grad_normed - mean_grad - normed * mean_mixed)).astype(BF16)


def head_mask(pair, head):
    lane = lax.broadcasted_iota(jnp.int32, pair.shape, 1)
    return jnp.where((lane < HEAD_DIM) == (head == 0), pair, jnp.zeros_like(pair))


def aligned(value, multiple):
    return pl.multiple_of(value, multiple)


def span(start, size):
    return pl.ds(aligned(start, size), size)


def call(kernel, name, in_specs, out_specs, out_shape, scratch, flops, aliases=None):
    return pl.pallas_call(
        kernel,
        in_specs=in_specs,
        out_specs=out_specs,
        out_shape=out_shape,
        scratch_shapes=scratch,
        compiler_params=pltpu.CompilerParams(vmem_limit_bytes=KERNEL_MIB << 20),
        cost_estimate=pl.CostEstimate(flops=flops, bytes_accessed=1 << 20, transcendentals=0),
        input_output_aliases=aliases or {},
        name=name,
    )


BATCH, SLOT, FIRST, OTHERS, EXTRA, ODD = range(6)


def over_rows(count, body):
    def step(index, carry):
        body(span(index * NORM_ROWS, NORM_ROWS))
        return carry

    lax.fori_loop(0, count // NORM_ROWS, step, 0)


def shifted(rows, by):
    return pl.ds(aligned(rows.start + by, HEAD_DIM), rows.size)


def scale_rows(batch, tokens, gain, scaled, into=0):
    half = tokens.shape[1] // 2

    def body(rows):
        normed, _ = normalise(tokens[rows, :])
        values = (normed * gain[...]).astype(BF16)
        place = shifted(rows, into)
        scaled[place, :half] = jnp.where(batch == 0, values[:, :half], values[:, half:])
        scaled[place, half:] = jnp.where(batch == 0, values[:, half:], values[:, :half])

    over_rows(tokens.shape[0], body)


def norm_backward_rows(tokens, back, gain, out, at=0):
    def body(rows):
        place = shifted(rows, at)
        out[place, :] = norm_backward(tokens[rows, :], back[place, :], gain[...])

    over_rows(tokens.shape[0], body)


def times_rows(batch, left, weights, out, rows, chunk):
    half = weights.shape[0] // 2
    per_half = half // chunk

    def columns(index, carry):
        place = jnp.where(index < per_half, batch, 1 - batch) * half + lax.rem(index, per_half) * chunk
        product = dot(left(), weights[span(index * chunk, chunk), :], 1, 1)
        out[rows, span(place, chunk)] = product.astype(out.dtype)
        return carry

    lax.fori_loop(0, 2 * per_half, columns, 0)


def times_halves(batch, left, rows, weights, out, chunk):
    half = weights.shape[0] // 2

    def columns(index, carry):
        at = span(index * chunk, chunk)
        product = dot(left[rows, span(batch * half, half)], weights[:half, at], 1, 0)
        product = product + dot(left[rows, span((1 - batch) * half, half)], weights[half:, at], 1, 0)
        out[:, at] = product.astype(BF16)
        return carry

    lax.fori_loop(0, weights.shape[1] // chunk, columns, 0)


def weight_rows(here, there, full, sems):
    half = here.shape[0]
    size = half // PIECES
    return tuple(
        pltpu.make_async_copy(
            source.at[pl.ds(piece * size, size)],
            full.at[pl.ds(place * half + piece * size, size)],
            sems.at[place * PIECES + piece],
        )
        for place, source in enumerate((here, there))
        for piece in range(PIECES)
    )


def multiply_columns(tokens, weights, out):
    def columns(index, carry):
        at = span(index * QUAD, QUAD)
        out[:, at] = dot(tokens[...], weights[at, :], 1, 1).astype(BF16)
        return carry

    lax.fori_loop(0, weights.shape[0] // QUAD, columns, 0)


def own_kernel(meta, tokens, cot, gain, o_here, scaled, upstream, *sent):
    scale_rows(meta[BATCH], tokens, gain, scaled)
    multiply_columns(cot, o_here, upstream)
    near = meta[SLOT] == 0

    def cut(source, out, if_near, if_far):
        start = aligned(jnp.where(near, if_near, if_far) * HEAD_DIM, HEAD_DIM)
        out[...] = source[pl.ds(start, out.shape[0]), :]

    for index, count in enumerate(COUNTS):
        cut(tokens, sent[2 * index], LEAD, WIN - count)
        cut(cot, sent[2 * index + 1], 0, WIN - count)


def own_tokens(meta, tokens, cot, gain, o_here):
    rows, channels = tokens.shape
    half = o_here.shape[0]
    shapes = [(rows, channels), (rows, half)]
    for count in COUNTS:
        shapes += [((count - LEAD) * HEAD_DIM, channels), (count * HEAD_DIM, channels)]
    return call(
        own_kernel,
        "own_tokens",
        [SCALAR] + [VECTOR] * 4,
        [VECTOR] * len(shapes),
        [jax.ShapeDtypeStruct(shape, BF16) for shape in shapes],
        [],
        rows * channels * channels,
    )(meta, tokens, cot, gain, o_here)


def rest_kernel(
    meta, x_first, gain, scaled_in, cot_in, w_here, w_there, o_here, o_there, qkv, upstream, w_full, o_full,
    scaled, cot, sems, w_sems, o_sems,
):
    half, width = w_here.shape
    rows = qkv.shape[0]
    first = pl.ds(aligned(meta[FIRST], HEAD_DIM), x_first.shape[0])
    chunk = 1024
    chunks = width // chunk
    scaled_copy = pltpu.make_async_copy(scaled_in, scaled.at[pl.ds(0, rows)], sems.at[0])
    later = (pltpu.make_async_copy(cot_in, cot, sems.at[1]),) + weight_rows(o_here, o_there, o_full, o_sems)

    def weight_copies(index):
        at = pl.ds(aligned(index * chunk, chunk), chunk)
        return (
            pltpu.make_async_copy(w_here.at[:, at], w_full.at[pl.ds(0, half), at], w_sems.at[0, index]),
            pltpu.make_async_copy(w_there.at[:, at], w_full.at[pl.ds(half, half), at], w_sems.at[1, index]),
        )

    scaled_copy.start()

    def start_weights(index, carry):
        for copy in weight_copies(index):
            copy.start()
        return carry

    lax.fori_loop(0, chunks, start_weights, 0)
    for copy in later:
        copy.start()
    scale_rows(meta[BATCH], x_first, gain, scaled, rows)
    scaled_copy.wait()

    def project(index, carry):
        for copy in weight_copies(index):
            copy.wait()
        at = pl.ds(aligned(index * chunk, chunk), chunk)
        product = dot(scaled[...], w_full[:, at], 1, 0).astype(BF16)
        qkv[:, at] = product[:rows]
        qkv[first, at] = product[rows:]
        return carry

    lax.fori_loop(0, chunks, project, 0)
    for copy in later:
        copy.wait()
    multiply_columns(cot, o_full.at[pl.ds(half, half)], upstream)


def rest_projection(meta, x_first, gain, scaled, cot, w_here, w_there, o_here, o_there):
    rows, channels = scaled.shape
    half, width = w_there.shape
    shapes = [(rows, width), (rows, half), (channels, width), (channels, channels)]
    return call(
        rest_kernel,
        "rest_projection",
        [SCALAR] + [VECTOR] * 2 + [ANYWHERE] * 6,
        [VECTOR] * 4,
        [jax.ShapeDtypeStruct(shape, BF16) for shape in shapes],
        [
            pltpu.VMEM((rows + x_first.shape[0], channels), BF16),
            pltpu.VMEM((rows, channels), BF16),
            pltpu.SemaphoreType.DMA((2,)),
            pltpu.SemaphoreType.DMA((2, width // 1024)),
            pltpu.SemaphoreType.DMA((2 * PIECES,)),
        ],
        rows * channels * (2 * width + channels),
    )(meta, x_first, gain, scaled, cot, w_here, w_there, o_here, o_there)


def forward_kernel(
    meta, x_others, gain, qkv_in, w_full, o_full,
    update_out, qkv, raised_out, inverse_out, attended,
    scaled, scores_a, scores_b, peak_a, peak_b, low_a, low_b, values_t, outs_t,
):
    batch = meta[BATCH]
    channels, width = w_full.shape
    rows = qkv.shape[0]
    count = update_out.shape[0]
    slot = pl.ds(aligned(meta[SLOT], HEAD_DIM), count)
    others = pl.ds(aligned(meta[OTHERS], HEAD_DIM), scaled.shape[0])
    extra = pl.ds(aligned(meta[EXTRA], HEAD_DIM), HEAD_DIM)
    chunk = 512
    scale_rows(batch, x_others, gain, scaled)

    def project(index, carry):
        at = span(index * chunk, chunk)
        own = qkv[extra, at]
        qkv[others, at] = dot(scaled[...], w_full[:, at], 1, 0).astype(BF16)

        @pl.when(meta[ODD] == 1)
        def _():
            qkv[extra, at] = own

        return carry

    lax.fori_loop(0, width // chunk, project, 0)

    def columns(part, pair):
        return span(part * channels + pair * PAIR, PAIR)

    def scores(pair, head, out, peak):
        query = qkv[:, columns(0, pair)] * BF16(HEAD_DIM ** -0.5)
        values = dot(qkv[:, columns(1, pair)], head_mask(query, head), 1, 1)
        out[...] = values
        peak[...] = jnp.max(values, axis=0, keepdims=True)

    def softmax(head, source, peak, low):
        top = peak[...]
        sums = jnp.zeros((8, rows), F32)
        for at in range(0, rows, FEW_ROWS):
            raised = jnp.exp(source[pl.ds(at, FEW_ROWS), :] - top)
            raised_out[head, pl.ds(at, FEW_ROWS), :] = raised
            sums = sums + jnp.sum(raised.reshape(FEW_ROWS // 8, 8, rows), axis=0)
        inverse = 1.0 / jnp.sum(sums, axis=0, keepdims=True)
        inverse_out[head] = inverse
        for at in range(0, rows, FEW_ROWS):
            low[pl.ds(at, FEW_ROWS), :] = (raised_out[head, pl.ds(at, FEW_ROWS), :] * inverse).astype(BF16)

    pairs = channels // PAIR
    scores(0, 0, scores_a, peak_a)

    def pair_of_heads(pair, carry):
        before = jnp.maximum(pair - 1, 0)
        after = jnp.minimum(pair + 1, pairs - 1)
        outs_t[HEAD_DIM:] = dot(values_t[HEAD_DIM:], low_b[...], 1, 0).astype(BF16)
        attended[:, columns(0, before)] = outs_t[...].T
        scores(pair, 1, scores_b, peak_b)
        softmax(2 * pair, scores_a, peak_a, low_a)
        values_t[...] = qkv[:, columns(2, pair)].T
        outs_t[:HEAD_DIM] = dot(values_t[:HEAD_DIM], low_a[...], 1, 0).astype(BF16)
        scores(after, 0, scores_a, peak_a)
        softmax(2 * pair + 1, scores_b, peak_b, low_b)
        return carry

    lax.fori_loop(0, pairs, pair_of_heads, 0, unroll=PAIRS_AT_ONCE)
    outs_t[HEAD_DIM:] = dot(values_t[HEAD_DIM:], low_b[...], 1, 0).astype(BF16)
    attended[:, columns(0, pairs - 1)] = outs_t[...].T
    times_halves(batch, attended, slot, o_full, update_out, chunk)


def forward(meta, x_others, gain, qkv, w_full, o_full):
    rows, width = qkv.shape
    channels = width // 3
    count = x_others.shape[0] + LEAD * HEAD_DIM
    heads = channels // HEAD_DIM
    return call(
        forward_kernel,
        "forward",
        [SCALAR] + [VECTOR] * 5,
        [VECTOR] * 5,
        [
            jax.ShapeDtypeStruct((count, channels), BF16),
            jax.ShapeDtypeStruct((rows, width), BF16),
            jax.ShapeDtypeStruct((heads, rows, rows), F32),
            jax.ShapeDtypeStruct((heads, 1, rows), F32),
            jax.ShapeDtypeStruct((rows, channels), BF16),
        ],
        [
            pltpu.VMEM(x_others.shape, BF16),
            pltpu.VMEM((rows, rows), F32),
            pltpu.VMEM((rows, rows), F32),
            pltpu.VMEM((1, rows), F32),
            pltpu.VMEM((1, rows), F32),
            pltpu.VMEM((rows, rows), BF16),
            pltpu.VMEM((rows, rows), BF16),
            pltpu.VMEM((PAIR, rows), BF16),
            pltpu.VMEM((PAIR, rows), BF16),
        ],
        12 * 10 ** 9,
        aliases={3: 1},
    )(meta, x_others, gain, qkv, w_full, o_full)


def backward_kernel(meta, *refs, width, begins, ends):
    refs = list(refs)

    def take(count):
        taken = refs[:count]
        del refs[:count]
        return taken

    qkv, raised, inverse, u_here, u_there = take(5)
    if not begins:
        dk_before, dv_before, _ = take(3)
    if ends:
        x_first, x_others, c_slot, gain, w_full, o_full = take(6)
        (grad_out,) = take(1)
    else:
        dk_out, dv_out = take(2)
    (
        grad_qkv,
        upstream, grads_a, grads_b, sum_a, sum_b, scores_a, scores_b, low_a, low_b, keys_t, dq_t, dk_sum, dv_sum,
    ) = take(14)
    batch = meta[BATCH]
    rows = qkv.shape[0]
    half = u_here.shape[1]
    channels = 2 * half
    slot_start = meta[SLOT]
    if width == rows:
        start = 0
    else:
        start = jnp.where((slot_start == 0) == ends, 0, width)
    tokens = pl.ds(aligned(start, width), width)
    here, there = span(batch * half, half), span((1 - batch) * half, half)
    upstream[:, here] = u_here[tokens, :]
    upstream[:, there] = u_there[tokens, :]

    if ends:
        count = c_slot.shape[0]
        place = pl.ds(aligned(slot_start - start, HEAD_DIM), count)
        times_rows(batch, lambda: c_slot[...], o_full, upstream, place, 2 * QUAD)

        @pl.when(meta[ODD] == 1)
        def _():
            local = pl.ds(aligned(meta[EXTRA] - start, HEAD_DIM), HEAD_DIM)
            extra = pl.ds(aligned(meta[EXTRA], HEAD_DIM), HEAD_DIM)
            upstream[local, here] = u_here[extra, :]
            upstream[local, there] = u_there[extra, :]

    def columns(part, pair):
        return span(part * channels + pair * PAIR, PAIR)

    def grad_probs(pair, head, out, row_sum):
        values = head_mask(qkv[:, columns(2, pair)], head)
        grads = dot(values, upstream[:, columns(0, pair)], 1, 1)
        out[...] = grads
        index = 2 * pair + head
        row_sum[...] = jnp.sum(grads * raised[index, :, tokens], axis=0, keepdims=True) * inverse[index, :, tokens]

    def score_grads(head, source, row_sum, scores, low):
        total = row_sum[...]
        scale = inverse[head, :, tokens]
        for at in range(0, rows, ROW_CHUNK):
            part = pl.ds(at, ROW_CHUNK)
            soft = raised[head, part, tokens] * scale
            low[part, :] = soft.astype(BF16)
            scores[part, :] = (soft * (source[part, :] - total)).astype(BF16)

    def products(pair, head, scores, low):
        from_keys = dot(scores[...], head_mask(qkv[tokens, columns(0, pair)], head), 1, 0)
        from_values = dot(low[...], head_mask(upstream[:, columns(0, pair)], head), 1, 0)
        part = slice(HEAD_DIM * head, HEAD_DIM * head + HEAD_DIM)
        dq_t[part] = (dot(keys_t[part], scores[...], 1, 0) * HEAD_DIM ** -0.5).astype(BF16)
        if head == 0:
            dk_sum[...] = from_keys
            dv_sum[...] = from_values
            return
        from_keys = dk_sum[...] + from_keys
        from_values = dv_sum[...] + from_values
        at = columns(0, pair)
        grad_qkv[tokens, at] = dq_t[...].T
        if not begins:
            from_keys = dk_before[:, at] + from_keys
            from_values = dv_before[:, at] + from_values
        if ends:
            grad_qkv[:, columns(1, pair)] = (from_keys * HEAD_DIM ** -0.5).astype(BF16)
            grad_qkv[:, columns(2, pair)] = from_values.astype(BF16)
        else:
            dk_out[:, at] = from_keys
            dv_out[:, at] = from_values

    pairs = channels // PAIR
    grad_probs(0, 0, grads_a, sum_a)

    def pair_of_heads(pair, carry):
        before = jnp.maximum(pair - 1, 0)
        after = jnp.minimum(pair + 1, pairs - 1)
        products(before, 1, scores_b, low_b)
        grad_probs(pair, 1, grads_b, sum_b)
        score_grads(2 * pair, grads_a, sum_a, scores_a, low_a)
        keys_t[...] = qkv[:, columns(1, pair)].T
        products(pair, 0, scores_a, low_a)
        grad_probs(after, 0, grads_a, sum_a)
        score_grads(2 * pair + 1, grads_b, sum_b, scores_b, low_b)
        return carry

    lax.fori_loop(0, pairs, pair_of_heads, 0, unroll=PAIRS_AT_ONCE)
    products(pairs - 1, 1, scores_b, low_b)
    if ends:
        (back,) = take(1)
        slot = pl.ds(aligned(slot_start, HEAD_DIM), count)
        times_rows(batch, lambda: grad_qkv[slot, :], w_full, back, slice(None), 2 * QUAD)
        norm_backward_rows(x_first, back, gain, grad_out, meta[FIRST] - slot_start)
        norm_backward_rows(x_others, back, gain, grad_out, meta[OTHERS] - slot_start)


def backward(meta, window, before=None, received=None, half=False):
    rows, width = window[0].shape
    channels = width // 3
    tokens = rows // 2 if half else rows
    begins, ends = before is None, received is not None
    square = (rows, tokens)
    operands = list(window) + list(before or ()) + list(received or ())
    sums = jax.ShapeDtypeStruct((rows, channels), F32)
    results = [jax.ShapeDtypeStruct((rows, width), BF16)]
    scratch = [
        pltpu.VMEM((tokens, channels), BF16),
        pltpu.VMEM(square, F32),
        pltpu.VMEM(square, F32),
        pltpu.VMEM((1, tokens), F32),
        pltpu.VMEM((1, tokens), F32),
        pltpu.VMEM(square, BF16),
        pltpu.VMEM(square, BF16),
        pltpu.VMEM(square, BF16),
        pltpu.VMEM(square, BF16),
        pltpu.VMEM((PAIR, rows), BF16),
        pltpu.VMEM((PAIR, tokens), BF16),
        pltpu.VMEM((rows, PAIR), F32),
        pltpu.VMEM((rows, PAIR), F32),
    ]
    if ends:
        count = received[2].shape[0]
        results = [jax.ShapeDtypeStruct((count, channels), BF16)] + results
        scratch = scratch + [pltpu.VMEM((count, channels), F32)]
    else:
        results = [sums, sums] + results
    return call(
        functools.partial(backward_kernel, width=tokens, begins=begins, ends=ends),
        "backward",
        [SCALAR] + [VECTOR] * len(operands),
        [VECTOR] * len(results),
        results,
        scratch,
        (10 if half else 20) * 10 ** 9,
        aliases=None if begins else {len(window) + len(before): len(results) - 1},
    )(meta, *operands)


def finish_kernel(
    meta, tokens, gain, attended, grad_qkv, received, w_full, o_full, update_out, grad_out,
    update, grad, back, sems,
):
    batch = meta[BATCH]
    rows, channels = tokens.shape
    count = received.shape[0]
    everything = slice(None)

    def copies(source, out, which):
        size = rows // PIECES
        return tuple(
            pltpu.make_async_copy(
                source.at[pl.ds(piece * size, size)], out.at[pl.ds(piece * size, size)], sems.at[which, piece]
            )
            for piece in range(PIECES)
        )

    times_halves(batch, attended, everything, o_full, update, 2 * QUAD)
    extra = pl.ds(aligned(meta[EXTRA], HEAD_DIM), HEAD_DIM)
    kept = update[extra, :]
    update[pl.ds(aligned(meta[SLOT], HEAD_DIM), count), :] = received[...]

    @pl.when(meta[ODD] == 1)
    def _():
        update[extra, :] = kept

    for copy in copies(update, update_out, 0):
        copy.start()
    times_rows(batch, lambda: grad_qkv[...], w_full, back, everything, 2 * QUAD)
    norm_backward_rows(tokens, back, gain, grad)
    for copy in copies(grad, grad_out, 1):
        copy.start()
    for copy in copies(update, update_out, 0) + copies(grad, grad_out, 1):
        copy.wait()


def finish(meta, tokens, gain, attended, grad_qkv, received, w_full, o_full):
    rows, channels = tokens.shape
    block = jax.ShapeDtypeStruct((rows, channels), BF16)
    return call(
        finish_kernel,
        "finish",
        [SCALAR] + [VECTOR] * 7,
        [ANYWHERE] * 2,
        [block] * 2,
        [
            pltpu.VMEM((rows, channels), BF16),
            pltpu.VMEM((rows, channels), BF16),
            pltpu.VMEM((rows, channels), F32),
            pltpu.SemaphoreType.DMA((2, PIECES)),
        ],
        8 * rows * channels * channels,
    )(meta, tokens, gain, attended, grad_qkv, received, w_full, o_full)


def merge_kernel(meta, grad_back, grad, out, sems):
    for index in range(grad_back.shape[0] // HEAD_DIM):
        start = aligned(meta[SLOT] + index * HEAD_DIM, HEAD_DIM)
        copy = pltpu.make_async_copy(
            grad_back.at[pl.ds(index * HEAD_DIM, HEAD_DIM)], out.at[pl.ds(start, HEAD_DIM)], sems.at[index]
        )
        wanted = jnp.logical_not((meta[ODD] == 1) & (start == meta[EXTRA]))
        pl.when(wanted)(copy.start)

    for index in range(grad_back.shape[0] // HEAD_DIM):
        start = aligned(meta[SLOT] + index * HEAD_DIM, HEAD_DIM)
        copy = pltpu.make_async_copy(
            grad_back.at[pl.ds(index * HEAD_DIM, HEAD_DIM)], out.at[pl.ds(start, HEAD_DIM)], sems.at[index]
        )
        wanted = jnp.logical_not((meta[ODD] == 1) & (start == meta[EXTRA]))
        pl.when(wanted)(copy.wait)


def merge(meta, grad_back, grad):
    return call(
        merge_kernel, "merge", [SCALAR, VECTOR, ANYWHERE], ANYWHERE, jax.ShapeDtypeStruct(grad.shape, BF16),
        [pltpu.SemaphoreType.DMA((HALF_WIN,))], 0, aliases={2: 0},
    )(meta, grad_back, grad)


def after_kernel(rows, earlier, out):
    pass


def after(rows, earlier):
    return call(
        after_kernel, "after", [ANYWHERE] * 2, ANYWHERE, jax.ShapeDtypeStruct(rows.shape, BF16), [], 0,
        aliases={0: 0},
    )(rows, earlier)


def exchange(rows, near, back):
    size = lax.axis_size("space")

    def along(by):
        return lax.ppermute(rows, "space", [(i, (i + by) % size) for i in range(size)])

    if size == 2 * YTILES:
        return along(YTILES)
    return jnp.where(near != back, along(-YTILES), along(YTILES))


def swapped(part):
    return lax.ppermute(part, "batch", [(0, 1), (1, 0)])


def shards(inputs, cotangent, offsets, w_qkv, w_out, gain):
    tiled_shape = inputs.shape
    channels = tiled_shape[-1]
    row = WIN * tiled_shape[4]
    tokens = inputs.reshape(-1, channels)
    cot = cotangent.reshape(-1, channels)
    gain = gain.reshape(1, channels)
    shift = offsets[0]
    near = shift <= HALF_WIN
    moved = jnp.minimum(shift, WIN - shift)
    batch = lax.axis_index("batch")

    first = jnp.where(near, 0, (WIN - LEAD) * row)
    o_there = swapped(w_out)
    w_there = swapped(w_qkv)
    x_first = exchange(lax.dynamic_slice_in_dim(tokens, first, LEAD * row, 0), near, False)

    def meta_of(count):
        slot = jnp.where(near, 0, (WIN - count) * row)
        others = jnp.where(near, LEAD * row, (WIN - count) * row)
        extra = jnp.where(near, (count - 1) * row, (WIN - count) * row)
        return jnp.stack([batch, slot, first, others, extra, moved < count]).astype(jnp.int32)

    scaled, u_here, *sent = own_tokens(meta_of(COUNTS[0]), tokens, cot, gain, w_out)

    def branch(count):
        def run(tokens, cot, x_first, scaled, u_here, weights, sent):
            meta = meta_of(count)
            x_sent, c_sent = sent[2 * COUNTS.index(count) :][:2]
            x_others = exchange(x_sent, near, False)
            c_slot = exchange(after(c_sent, x_others), near, False)
            qkv, u_there, w_full, o_full = rest_projection(meta, x_first, gain, scaled, cot, *weights)
            update_sent, window, raised, inverse, attended = forward(meta, x_others, gain, qkv, w_full, o_full)
            window = (window, raised, inverse, u_here, u_there)
            received = (x_first, x_others, c_slot, gain, w_full, o_full)
            update_back = exchange(after(update_sent, c_slot), near, True)
            if count in HALVED:
                before = backward(meta, window, half=True)
                grad_sent, grad_qkv = backward(meta, window, before, received, half=True)
            else:
                grad_sent, grad_qkv = backward(meta, window, received=received)
            grad_back = exchange(grad_sent, near, True)
            update, grad = finish(meta, tokens, gain, attended, grad_qkv, update_back, w_full, o_full)
            return update, merge(meta, grad_back, grad)

        return run

    update, grad = lax.switch(
        jnp.maximum(moved, COUNTS[0]) - COUNTS[0],
        [branch(count) for count in COUNTS],
        tokens, cot, x_first, scaled, u_here, (w_qkv, w_there, w_out, o_there), tuple(sent),
    )
    return (update.reshape(tiled_shape), grad.reshape(tiled_shape))


def solution(mesh):
    in_specs = (
        P(("groups", "batch"), "space", None, None, None, None),
        P(("groups", "batch"), "space", None, None, None, None),
        P(("groups", "batch")),
        P("batch", None),
        P("batch", None),
        P(),
    )
    out_specs = (
        P(("groups", "batch"), "space", None, None, None, None),
        P(("groups", "batch"), "space", None, None, None, None),
    )
    return jax.shard_map(shards, mesh=mesh, in_specs=in_specs, out_specs=out_specs, check_vma=False)
```

```python
import functools

import jax
import jax.numpy as jnp
from jax import lax
from jax.experimental import pallas as pl
from jax.experimental.pallas import tpu as pltpu
from jax.sharding import PartitionSpec as P

WIN = 8
YTILES = 4
HEAD_DIM = 64
EPS = 1e-05
PAIR = 2 * HEAD_DIM
QUAD = 4 * HEAD_DIM
HALF_WIN = WIN // 2
LEAD = 1
COUNTS = (2, 3, 4)
HALVED = ()
BF16 = jnp.bfloat16
F32 = jnp.float32
NORM_ROWS = 64
MANY_ROWS = 128
ROW_CHUNK = 64
FEW_ROWS = 16
PIECES = 4
KERNEL_MIB = 12
ANYWHERE = pl.BlockSpec(memory_space=pltpu.HBM)
VECTOR = pl.BlockSpec(memory_space=pltpu.VMEM)
SCALAR = pl.BlockSpec(memory_space=pltpu.SMEM)
NORM_ROWS = 64
MANY_ROWS = 128
ROW_CHUNK = 64
FEW_ROWS = 16
PIECES = 4
KERNEL_MIB = 12
PAIRS_AT_ONCE = 2


def dot(left, right, left_dim, right_dim):
    return lax.dot_general(
        left, right, (((left_dim,), (right_dim,)), ((), ())), preferred_element_type=F32
    )


def normalise(tokens):
    values32 = tokens.astype(F32)
    center = values32 - jnp.mean(values32, axis=-1, keepdims=True)
    inverse = lax.rsqrt(jnp.mean(center * center, axis=-1, keepdims=True) + EPS)
    return center * inverse, inverse


def norm_backward(tokens, grad_scaled, gain):
    normed, inverse = normalise(tokens)
    grad_normed = grad_scaled * gain
    mean_grad = jnp.mean(grad_normed, axis=-1, keepdims=True)
    mean_mixed = jnp.mean(grad_normed * normed, axis=-1, keepdims=True)
    return (inverse * (grad_normed - mean_grad - normed * mean_mixed)).astype(BF16)


def head_mask(pair, head):
    lane = lax.broadcasted_iota(jnp.int32, pair.shape, 1)
    return jnp.where((lane < HEAD_DIM) == (head == 0), pair, jnp.zeros_like(pair))


def aligned(value, multiple):
    return pl.multiple_of(value, multiple)


def span(start, size):
    return pl.ds(aligned(start, size), size)


def call(kernel, name, in_specs, out_specs, out_shape, scratch, flops, aliases=None):
    return pl.pallas_call(
        kernel,
        in_specs=in_specs,
        out_specs=out_specs,
        out_shape=out_shape,
        scratch_shapes=scratch,
        compiler_params=pltpu.CompilerParams(vmem_limit_bytes=KERNEL_MIB << 20),
        cost_estimate=pl.CostEstimate(flops=flops, bytes_accessed=1 << 20, transcendentals=0),
        input_output_aliases=aliases or {},
        name=name,
    )


BATCH, SLOT, FIRST, OTHERS, EXTRA, ODD = range(6)


def over_rows(count, body):
    size = MANY_ROWS if count % MANY_ROWS == 0 else NORM_ROWS

    def step(index, carry):
        body(span(index * size, size))
        return carry

    lax.fori_loop(0, count // size, step, 0)


def shifted(rows, by):
    return pl.ds(aligned(rows.start + by, HEAD_DIM), rows.size)


def scale_rows(batch, tokens, gain, scaled, into=0):
    half = tokens.shape[1] // 2

    def body(rows):
        normed, _ = normalise(tokens[rows, :])
        values = (normed * gain[...]).astype(BF16)
        place = shifted(rows, into)
        scaled[place, :half] = jnp.where(batch == 0, values[:, :half], values[:, half:])
        scaled[place, half:] = jnp.where(batch == 0, values[:, half:], values[:, :half])

    over_rows(tokens.shape[0], body)


def norm_backward_rows(tokens, back, gain, out, at=0):
    def body(rows):
        place = shifted(rows, at)
        out[place, :] = norm_backward(tokens[rows, :], back[place, :], gain[...])

    over_rows(tokens.shape[0], body)


def times_rows(batch, left, weights, out, rows, chunk):
    half = weights.shape[0] // 2
    per_half = half // chunk

    def columns(index, carry):
        place = jnp.where(index < per_half, batch, 1 - batch) * half + lax.rem(index, per_half) * chunk
        product = dot(left(), weights[span(index * chunk, chunk), :], 1, 1)
        out[rows, span(place, chunk)] = product.astype(out.dtype)
        return carry

    lax.fori_loop(0, 2 * per_half, columns, 0)


def times_halves(batch, left, rows, weights, out, chunk):
    half = weights.shape[0] // 2

    def columns(index, carry):
        at = span(index * chunk, chunk)
        product = dot(left[rows, span(batch * half, half)], weights[:half, at], 1, 0)
        product = product + dot(left[rows, span((1 - batch) * half, half)], weights[half:, at], 1, 0)
        out[:, at] = product.astype(BF16)
        return carry

    lax.fori_loop(0, weights.shape[1] // chunk, columns, 0)


def weight_rows(here, there, full, sems):
    half = here.shape[0]
    size = half // PIECES
    return tuple(
        pltpu.make_async_copy(
            source.at[pl.ds(piece * size, size)],
            full.at[pl.ds(place * half + piece * size, size)],
            sems.at[place * PIECES + piece],
        )
        for place, source in enumerate((here, there))
        for piece in range(PIECES)
    )


def multiply_columns(tokens, weights, out):
    def columns(index, carry):
        at = span(index * QUAD, QUAD)
        out[:, at] = dot(tokens[...], weights[at, :], 1, 1).astype(BF16)
        return carry

    lax.fori_loop(0, weights.shape[0] // QUAD, columns, 0)


def own_kernel(meta, tokens, cot, gain, o_here, scaled, upstream, *sent):
    scale_rows(meta[BATCH], tokens, gain, scaled)
    multiply_columns(cot, o_here, upstream)
    near = meta[SLOT] == 0

    def cut(source, out, if_near, if_far):
        start = aligned(jnp.where(near, if_near, if_far) * HEAD_DIM, HEAD_DIM)
        out[...] = source[pl.ds(start, out.shape[0]), :]

    for index, count in enumerate(COUNTS):
        cut(tokens, sent[2 * index], LEAD, WIN - count)
        cut(cot, sent[2 * index + 1], 0, WIN - count)


def own_tokens(meta, tokens, cot, gain, o_here):
    rows, channels = tokens.shape
    half = o_here.shape[0]
    shapes = [(rows, channels), (rows, half)]
    for count in COUNTS:
        shapes += [((count - LEAD) * HEAD_DIM, channels), (count * HEAD_DIM, channels)]
    return call(
        own_kernel,
        "own_tokens",
        [SCALAR] + [VECTOR] * 4,
        [VECTOR] * len(shapes),
        [jax.ShapeDtypeStruct(shape, BF16) for shape in shapes],
        [],
        rows * channels * channels,
    )(meta, tokens, cot, gain, o_here)


def rest_kernel(
    meta, x_first, gain, scaled_in, cot_in, w_here, w_there, o_here, o_there, qkv, upstream, w_full, o_full,
    scaled, cot, sems, w_sems, o_sems,
):
    half, width = w_here.shape
    rows = qkv.shape[0]
    first = pl.ds(aligned(meta[FIRST], HEAD_DIM), x_first.shape[0])
    chunk = 1024
    chunks = width // chunk
    scaled_copy = pltpu.make_async_copy(scaled_in, scaled.at[pl.ds(0, rows)], sems.at[0])
    later = (pltpu.make_async_copy(cot_in, cot, sems.at[1]),) + weight_rows(o_here, o_there, o_full, o_sems)

    def weight_copies(index):
        at = pl.ds(aligned(index * chunk, chunk), chunk)
        return (
            pltpu.make_async_copy(w_here.at[:, at], w_full.at[pl.ds(0, half), at], w_sems.at[0, index]),
            pltpu.make_async_copy(w_there.at[:, at], w_full.at[pl.ds(half, half), at], w_sems.at[1, index]),
        )

    scaled_copy.start()

    def start_weights(index, carry):
        for copy in weight_copies(index):
            copy.start()
        return carry

    lax.fori_loop(0, chunks, start_weights, 0)
    for copy in later:
        copy.start()
    scale_rows(meta[BATCH], x_first, gain, scaled, rows)
    scaled_copy.wait()

    def project(index, carry):
        for copy in weight_copies(index):
            copy.wait()
        at = pl.ds(aligned(index * chunk, chunk), chunk)
        product = dot(scaled[...], w_full[:, at], 1, 0).astype(BF16)
        qkv[:, at] = product[:rows]
        qkv[first, at] = product[rows:]
        return carry

    lax.fori_loop(0, chunks, project, 0)
    for copy in later:
        copy.wait()
    multiply_columns(cot, o_full.at[pl.ds(half, half)], upstream)


def rest_projection(meta, x_first, gain, scaled, cot, w_here, w_there, o_here, o_there):
    rows, channels = scaled.shape
    half, width = w_there.shape
    shapes = [(rows, width), (rows, half), (channels, width), (channels, channels)]
    return call(
        rest_kernel,
        "rest_projection",
        [SCALAR] + [VECTOR] * 2 + [ANYWHERE] * 6,
        [VECTOR] * 4,
        [jax.ShapeDtypeStruct(shape, BF16) for shape in shapes],
        [
            pltpu.VMEM((rows + x_first.shape[0], channels), BF16),
            pltpu.VMEM((rows, channels), BF16),
            pltpu.SemaphoreType.DMA((2,)),
            pltpu.SemaphoreType.DMA((2, width // 1024)),
            pltpu.SemaphoreType.DMA((2 * PIECES,)),
        ],
        rows * channels * (2 * width + channels),
    )(meta, x_first, gain, scaled, cot, w_here, w_there, o_here, o_there)


def forward_kernel(
    meta, x_others, gain, qkv_in, w_full, o_full,
    update_out, qkv, raised_out, inverse_out, attended,
    scaled, scores_a, scores_b, peak_a, peak_b, low_a, low_b, values_t, outs_t,
):
    batch = meta[BATCH]
    channels, width = w_full.shape
    rows = qkv.shape[0]
    count = update_out.shape[0]
    slot = pl.ds(aligned(meta[SLOT], HEAD_DIM), count)
    others = pl.ds(aligned(meta[OTHERS], HEAD_DIM), scaled.shape[0])
    extra = pl.ds(aligned(meta[EXTRA], HEAD_DIM), HEAD_DIM)
    chunk = 512
    scale_rows(batch, x_others, gain, scaled)

    def project(index, carry):
        at = span(index * chunk, chunk)
        own = qkv[extra, at]
        qkv[others, at] = dot(scaled[...], w_full[:, at], 1, 0).astype(BF16)

        @pl.when(meta[ODD] == 1)
        def _():
            qkv[extra, at] = own

        return carry

    lax.fori_loop(0, width // chunk, project, 0)

    def columns(part, pair):
        return span(part * channels + pair * PAIR, PAIR)

    def scores(pair, head, out, peak):
        query = qkv[:, columns(0, pair)] * BF16(HEAD_DIM ** -0.5)
        values = dot(qkv[:, columns(1, pair)], head_mask(query, head), 1, 1)
        out[...] = values
        peak[...] = jnp.max(values, axis=0, keepdims=True)

    def softmax(head, source, peak, low):
        top = peak[...]
        sums = jnp.zeros((8, rows), F32)
        for at in range(0, rows, FEW_ROWS):
            raised = jnp.exp(source[pl.ds(at, FEW_ROWS), :] - top)
            raised_out[head, pl.ds(at, FEW_ROWS), :] = raised
            sums = sums + jnp.sum(raised.reshape(FEW_ROWS // 8, 8, rows), axis=0)
        inverse = 1.0 / jnp.sum(sums, axis=0, keepdims=True)
        inverse_out[head] = inverse
        for at in range(0, rows, FEW_ROWS):
            low[pl.ds(at, FEW_ROWS), :] = (raised_out[head, pl.ds(at, FEW_ROWS), :] * inverse).astype(BF16)

    pairs = channels // PAIR
    scores(0, 0, scores_a, peak_a)

    def pair_of_heads(pair, carry):
        before = jnp.maximum(pair - 1, 0)
        after = jnp.minimum(pair + 1, pairs - 1)
        outs_t[HEAD_DIM:] = dot(values_t[HEAD_DIM:], low_b[...], 1, 0).astype(BF16)
        attended[:, columns(0, before)] = outs_t[...].T
        scores(pair, 1, scores_b, peak_b)
        softmax(2 * pair, scores_a, peak_a, low_a)
        values_t[...] = qkv[:, columns(2, pair)].T
        outs_t[:HEAD_DIM] = dot(values_t[:HEAD_DIM], low_a[...], 1, 0).astype(BF16)
        scores(after, 0, scores_a, peak_a)
        softmax(2 * pair + 1, scores_b, peak_b, low_b)
        return carry

    lax.fori_loop(0, pairs, pair_of_heads, 0, unroll=PAIRS_AT_ONCE)
    outs_t[HEAD_DIM:] = dot(values_t[HEAD_DIM:], low_b[...], 1, 0).astype(BF16)
    attended[:, columns(0, pairs - 1)] = outs_t[...].T
    times_halves(batch, attended, slot, o_full, update_out, chunk)


def forward(meta, x_others, gain, qkv, w_full, o_full):
    rows, width = qkv.shape
    channels = width // 3
    count = x_others.shape[0] + LEAD * HEAD_DIM
    heads = channels // HEAD_DIM
    return call(
        forward_kernel,
        "forward",
        [SCALAR] + [VECTOR] * 5,
        [VECTOR] * 5,
        [
            jax.ShapeDtypeStruct((count, channels), BF16),
            jax.ShapeDtypeStruct((rows, width), BF16),
            jax.ShapeDtypeStruct((heads, rows, rows), F32),
            jax.ShapeDtypeStruct((heads, 1, rows), F32),
            jax.ShapeDtypeStruct((rows, channels), BF16),
        ],
        [
            pltpu.VMEM(x_others.shape, BF16),
            pltpu.VMEM((rows, rows), F32),
            pltpu.VMEM((rows, rows), F32),
            pltpu.VMEM((1, rows), F32),
            pltpu.VMEM((1, rows), F32),
            pltpu.VMEM((rows, rows), BF16),
            pltpu.VMEM((rows, rows), BF16),
            pltpu.VMEM((PAIR, rows), BF16),
            pltpu.VMEM((PAIR, rows), BF16),
        ],
        12 * 10 ** 9,
        aliases={3: 1},
    )(meta, x_others, gain, qkv, w_full, o_full)


def backward_kernel(meta, *refs, width, begins, ends):
    refs = list(refs)

    def take(count):
        taken = refs[:count]
        del refs[:count]
        return taken

    qkv, raised, inverse, u_here, u_there = take(5)
    if not begins:
        dk_before, dv_before, _ = take(3)
    if ends:
        x_first, x_others, c_slot, gain, w_full, o_full = take(6)
        (grad_out,) = take(1)
    else:
        dk_out, dv_out = take(2)
    (
        grad_qkv,
        upstream, grads_a, grads_b, sum_a, sum_b, scores_a, scores_b, low_a, low_b, keys_t, dq_t, dk_sum, dv_sum,
    ) = take(14)
    batch = meta[BATCH]
    rows = qkv.shape[0]
    half = u_here.shape[1]
    channels = 2 * half
    slot_start = meta[SLOT]
    if width == rows:
        start = 0
    else:
        start = jnp.where((slot_start == 0) == ends, 0, width)
    tokens = pl.ds(aligned(start, width), width)
    here, there = span(batch * half, half), span((1 - batch) * half, half)
    upstream[:, here] = u_here[tokens, :]
    upstream[:, there] = u_there[tokens, :]

    if ends:
        count = c_slot.shape[0]
        place = pl.ds(aligned(slot_start - start, HEAD_DIM), count)
        times_rows(batch, lambda: c_slot[...], o_full, upstream, place, 2 * QUAD)

        @pl.when(meta[ODD] == 1)
        def _():
            local = pl.ds(aligned(meta[EXTRA] - start, HEAD_DIM), HEAD_DIM)
            extra = pl.ds(aligned(meta[EXTRA], HEAD_DIM), HEAD_DIM)
            upstream[local, here] = u_here[extra, :]
            upstream[local, there] = u_there[extra, :]

    def columns(part, pair):
        return span(part * channels + pair * PAIR, PAIR)

    def grad_probs(pair, head, out, row_sum):
        values = head_mask(qkv[:, columns(2, pair)], head)
        grads = dot(values, upstream[:, columns(0, pair)], 1, 1)
        out[...] = grads
        index = 2 * pair + head
        row_sum[...] = jnp.sum(grads * raised[index, :, tokens], axis=0, keepdims=True) * inverse[index, :, tokens]

    def score_grads(head, source, row_sum, scores, low):
        total = row_sum[...]
        scale = inverse[head, :, tokens]
        for at in range(0, rows, ROW_CHUNK):
            part = pl.ds(at, ROW_CHUNK)
            soft = raised[head, part, tokens] * scale
            low[part, :] = soft.astype(BF16)
            scores[part, :] = (soft * (source[part, :] - total)).astype(BF16)

    def products(pair, head, scores, low):
        from_keys = dot(scores[...], head_mask(qkv[tokens, columns(0, pair)], head), 1, 0)
        from_values = dot(low[...], head_mask(upstream[:, columns(0, pair)], head), 1, 0)
        part = slice(HEAD_DIM * head, HEAD_DIM * head + HEAD_DIM)
        dq_t[part] = (dot(keys_t[part], scores[...], 1, 0) * HEAD_DIM ** -0.5).astype(BF16)
        if head == 0:
            dk_sum[...] = from_keys
            dv_sum[...] = from_values
            return
        from_keys = dk_sum[...] + from_keys
        from_values = dv_sum[...] + from_values
        at = columns(0, pair)
        grad_qkv[tokens, at] = dq_t[...].T
        if not begins:
            from_keys = dk_before[:, at] + from_keys
            from_values = dv_before[:, at] + from_values
        if ends:
            grad_qkv[:, columns(1, pair)] = (from_keys * HEAD_DIM ** -0.5).astype(BF16)
            grad_qkv[:, columns(2, pair)] = from_values.astype(BF16)
        else:
            dk_out[:, at] = from_keys
            dv_out[:, at] = from_values

    pairs = channels // PAIR
    grad_probs(0, 0, grads_a, sum_a)

    def pair_of_heads(pair, carry):
        before = jnp.maximum(pair - 1, 0)
        after = jnp.minimum(pair + 1, pairs - 1)
        products(before, 1, scores_b, low_b)
        grad_probs(pair, 1, grads_b, sum_b)
        score_grads(2 * pair, grads_a, sum_a, scores_a, low_a)
        keys_t[...] = qkv[:, columns(1, pair)].T
        products(pair, 0, scores_a, low_a)
        grad_probs(after, 0, grads_a, sum_a)
        score_grads(2 * pair + 1, grads_b, sum_b, scores_b, low_b)
        return carry

    lax.fori_loop(0, pairs, pair_of_heads, 0, unroll=PAIRS_AT_ONCE)
    products(pairs - 1, 1, scores_b, low_b)
    if ends:
        (back,) = take(1)
        slot = pl.ds(aligned(slot_start, HEAD_DIM), count)
        times_rows(batch, lambda: grad_qkv[slot, :], w_full, back, slice(None), 2 * QUAD)
        norm_backward_rows(x_first, back, gain, grad_out, meta[FIRST] - slot_start)
        norm_backward_rows(x_others, back, gain, grad_out, meta[OTHERS] - slot_start)


def backward(meta, window, before=None, received=None, half=False):
    rows, width = window[0].shape
    channels = width // 3
    tokens = rows // 2 if half else rows
    begins, ends = before is None, received is not None
    square = (rows, tokens)
    operands = list(window) + list(before or ()) + list(received or ())
    sums = jax.ShapeDtypeStruct((rows, channels), F32)
    results = [jax.ShapeDtypeStruct((rows, width), BF16)]
    scratch = [
        pltpu.VMEM((tokens, channels), BF16),
        pltpu.VMEM(square, F32),
        pltpu.VMEM(square, F32),
        pltpu.VMEM((1, tokens), F32),
        pltpu.VMEM((1, tokens), F32),
        pltpu.VMEM(square, BF16),
        pltpu.VMEM(square, BF16),
        pltpu.VMEM(square, BF16),
        pltpu.VMEM(square, BF16),
        pltpu.VMEM((PAIR, rows), BF16),
        pltpu.VMEM((PAIR, tokens), BF16),
        pltpu.VMEM((rows, PAIR), F32),
        pltpu.VMEM((rows, PAIR), F32),
    ]
    if ends:
        count = received[2].shape[0]
        results = [jax.ShapeDtypeStruct((count, channels), BF16)] + results
        scratch = scratch + [pltpu.VMEM((count, channels), F32)]
    else:
        results = [sums, sums] + results
    return call(
        functools.partial(backward_kernel, width=tokens, begins=begins, ends=ends),
        "backward",
        [SCALAR] + [VECTOR] * len(operands),
        [VECTOR] * len(results),
        results,
        scratch,
        (10 if half else 20) * 10 ** 9,
        aliases=None if begins else {len(window) + len(before): len(results) - 1},
    )(meta, *operands)


def finish_kernel(
    meta, tokens, gain, attended, grad_qkv, received, w_full, o_full, update_out, grad_out,
    update, grad, back, sems,
):
    batch = meta[BATCH]
    rows, channels = tokens.shape
    count = received.shape[0]
    everything = slice(None)

    def copies(source, out, which):
        size = rows // PIECES
        return tuple(
            pltpu.make_async_copy(
                source.at[pl.ds(piece * size, size)], out.at[pl.ds(piece * size, size)], sems.at[which, piece]
            )
            for piece in range(PIECES)
        )

    times_halves(batch, attended, everything, o_full, update, 2 * QUAD)
    extra = pl.ds(aligned(meta[EXTRA], HEAD_DIM), HEAD_DIM)
    kept = update[extra, :]
    update[pl.ds(aligned(meta[SLOT], HEAD_DIM), count), :] = received[...]

    @pl.when(meta[ODD] == 1)
    def _():
        update[extra, :] = kept

    for copy in copies(update, update_out, 0):
        copy.start()
    times_rows(batch, lambda: grad_qkv[...], w_full, back, everything, 2 * QUAD)
    norm_backward_rows(tokens, back, gain, grad)
    for copy in copies(grad, grad_out, 1):
        copy.start()
    for copy in copies(update, update_out, 0) + copies(grad, grad_out, 1):
        copy.wait()


def finish(meta, tokens, gain, attended, grad_qkv, received, w_full, o_full):
    rows, channels = tokens.shape
    block = jax.ShapeDtypeStruct((rows, channels), BF16)
    return call(
        finish_kernel,
        "finish",
        [SCALAR] + [VECTOR] * 7,
        [ANYWHERE] * 2,
        [block] * 2,
        [
            pltpu.VMEM((rows, channels), BF16),
            pltpu.VMEM((rows, channels), BF16),
            pltpu.VMEM((rows, channels), F32),
            pltpu.SemaphoreType.DMA((2, PIECES)),
        ],
        8 * rows * channels * channels,
    )(meta, tokens, gain, attended, grad_qkv, received, w_full, o_full)


def merge_kernel(meta, grad_back, grad, out, sems):
    for index in range(grad_back.shape[0] // HEAD_DIM):
        start = aligned(meta[SLOT] + index * HEAD_DIM, HEAD_DIM)
        copy = pltpu.make_async_copy(
            grad_back.at[pl.ds(index * HEAD_DIM, HEAD_DIM)], out.at[pl.ds(start, HEAD_DIM)], sems.at[index]
        )
        wanted = jnp.logical_not((meta[ODD] == 1) & (start == meta[EXTRA]))
        pl.when(wanted)(copy.start)

    for index in range(grad_back.shape[0] // HEAD_DIM):
        start = aligned(meta[SLOT] + index * HEAD_DIM, HEAD_DIM)
        copy = pltpu.make_async_copy(
            grad_back.at[pl.ds(index * HEAD_DIM, HEAD_DIM)], out.at[pl.ds(start, HEAD_DIM)], sems.at[index]
        )
        wanted = jnp.logical_not((meta[ODD] == 1) & (start == meta[EXTRA]))
        pl.when(wanted)(copy.wait)


def merge(meta, grad_back, grad):
    return call(
        merge_kernel, "merge", [SCALAR, VECTOR, ANYWHERE], ANYWHERE, jax.ShapeDtypeStruct(grad.shape, BF16),
        [pltpu.SemaphoreType.DMA((HALF_WIN,))], 0, aliases={2: 0},
    )(meta, grad_back, grad)


def after_kernel(rows, earlier, out):
    pass


def after(rows, earlier):
    return call(
        after_kernel, "after", [ANYWHERE] * 2, ANYWHERE, jax.ShapeDtypeStruct(rows.shape, BF16), [], 0,
        aliases={0: 0},
    )(rows, earlier)


def exchange(rows, near, back):
    size = lax.axis_size("space")

    def along(by):
        return lax.ppermute(rows, "space", [(i, (i + by) % size) for i in range(size)])

    if size == 2 * YTILES:
        return along(YTILES)
    return jnp.where(near != back, along(-YTILES), along(YTILES))


def swapped(part):
    return lax.ppermute(part, "batch", [(0, 1), (1, 0)])


def shards(inputs, cotangent, offsets, w_qkv, w_out, gain):
    tiled_shape = inputs.shape
    channels = tiled_shape[-1]
    row = WIN * tiled_shape[4]
    tokens = inputs.reshape(-1, channels)
    cot = cotangent.reshape(-1, channels)
    gain = gain.reshape(1, channels)
    shift = offsets[0]
    near = shift <= HALF_WIN
    moved = jnp.minimum(shift, WIN - shift)
    batch = lax.axis_index("batch")

    first = jnp.where(near, 0, (WIN - LEAD) * row)
    o_there = swapped(w_out)
    w_there = swapped(w_qkv)
    x_first = exchange(lax.dynamic_slice_in_dim(tokens, first, LEAD * row, 0), near, False)

    def meta_of(count):
        slot = jnp.where(near, 0, (WIN - count) * row)
        others = jnp.where(near, LEAD * row, (WIN - count) * row)
        extra = jnp.where(near, (count - 1) * row, (WIN - count) * row)
        return jnp.stack([batch, slot, first, others, extra, moved < count]).astype(jnp.int32)

    scaled, u_here, *sent = own_tokens(meta_of(COUNTS[0]), tokens, cot, gain, w_out)

    def branch(count):
        def run(tokens, cot, x_first, scaled, u_here, weights, sent):
            meta = meta_of(count)
            x_sent, c_sent = sent[2 * COUNTS.index(count) :][:2]
            x_others = exchange(x_sent, near, False)
            c_slot = exchange(after(c_sent, x_others), near, False)
            qkv, u_there, w_full, o_full = rest_projection(meta, x_first, gain, scaled, cot, *weights)
            update_sent, window, raised, inverse, attended = forward(meta, x_others, gain, qkv, w_full, o_full)
            window = (window, raised, inverse, u_here, u_there)
            received = (x_first, x_others, c_slot, gain, w_full, o_full)
            update_back = exchange(after(update_sent, c_slot), near, True)
            if count in HALVED:
                before = backward(meta, window, half=True)
                grad_sent, grad_qkv = backward(meta, window, before, received, half=True)
            else:
                grad_sent, grad_qkv = backward(meta, window, received=received)
            grad_back = exchange(grad_sent, near, True)
            update, grad = finish(meta, tokens, gain, attended, grad_qkv, update_back, w_full, o_full)
            return update, merge(meta, grad_back, grad)

        return run

    update, grad = lax.switch(
        jnp.maximum(moved, COUNTS[0]) - COUNTS[0],
        [branch(count) for count in COUNTS],
        tokens, cot, x_first, scaled, u_here, (w_qkv, w_there, w_out, o_there), tuple(sent),
    )
    return (update.reshape(tiled_shape), grad.reshape(tiled_shape))


def solution(mesh):
    in_specs = (
        P(("groups", "batch"), "space", None, None, None, None),
        P(("groups", "batch"), "space", None, None, None, None),
        P(("groups", "batch")),
        P("batch", None),
        P("batch", None),
        P(),
    )
    out_specs = (
        P(("groups", "batch"), "space", None, None, None, None),
        P(("groups", "batch"), "space", None, None, None, None),
    )
    return jax.shard_map(shards, mesh=mesh, in_specs=in_specs, out_specs=out_specs, check_vma=False)
```

```python
import functools

import jax
import jax.numpy as jnp
from jax import lax
from jax.experimental import pallas as pl
from jax.experimental.pallas import tpu as pltpu
from jax.sharding import PartitionSpec as P

WIN = 8
YTILES = 4
HEAD_DIM = 64
EPS = 1e-05
PAIR = 2 * HEAD_DIM
QUAD = 4 * HEAD_DIM
HALF_WIN = WIN // 2
LEAD = 1
COUNTS = (2, 3, 4)
HALVED = ()
BF16 = jnp.bfloat16
F32 = jnp.float32
NORM_ROWS = 64
MANY_ROWS = 128
ROW_CHUNK = 64
FEW_ROWS = 16
PIECES = 4
KERNEL_MIB = 12
ANYWHERE = pl.BlockSpec(memory_space=pltpu.HBM)
VECTOR = pl.BlockSpec(memory_space=pltpu.VMEM)
SCALAR = pl.BlockSpec(memory_space=pltpu.SMEM)
NORM_ROWS = 64
MANY_ROWS = 128
ROW_CHUNK = 64
FEW_ROWS = 16
PIECES = 4
KERNEL_MIB = 12
PAIRS_AT_ONCE = 2


def dot(left, right, left_dim, right_dim):
    return lax.dot_general(
        left, right, (((left_dim,), (right_dim,)), ((), ())), preferred_element_type=F32
    )


def normalise(tokens):
    values32 = tokens.astype(F32)
    center = values32 - jnp.mean(values32, axis=-1, keepdims=True)
    inverse = lax.rsqrt(jnp.mean(center * center, axis=-1, keepdims=True) + EPS)
    return center * inverse, inverse


def norm_backward(tokens, grad_scaled, gain):
    normed, inverse = normalise(tokens)
    grad_normed = grad_scaled * gain
    mean_grad = jnp.mean(grad_normed, axis=-1, keepdims=True)
    mean_mixed = jnp.mean(grad_normed * normed, axis=-1, keepdims=True)
    return (inverse * (grad_normed - mean_grad - normed * mean_mixed)).astype(BF16)


def head_mask(pair, head):
    lane = lax.broadcasted_iota(jnp.int32, pair.shape, 1)
    return jnp.where((lane < HEAD_DIM) == (head == 0), pair, jnp.zeros_like(pair))


def aligned(value, multiple):
    return pl.multiple_of(value, multiple)


def span(start, size):
    return pl.ds(aligned(start, size), size)


def call(kernel, name, in_specs, out_specs, out_shape, scratch, flops, aliases=None):
    return pl.pallas_call(
        kernel,
        in_specs=in_specs,
        out_specs=out_specs,
        out_shape=out_shape,
        scratch_shapes=scratch,
        compiler_params=pltpu.CompilerParams(vmem_limit_bytes=KERNEL_MIB << 20),
        cost_estimate=pl.CostEstimate(flops=flops, bytes_accessed=1 << 20, transcendentals=0),
        input_output_aliases=aliases or {},
        name=name,
    )


BATCH, SLOT, FIRST, OTHERS, EXTRA, ODD = range(6)


def over_rows(count, body):
    size = MANY_ROWS if count % MANY_ROWS == 0 else NORM_ROWS

    def step(index, carry):
        body(span(index * size, size))
        return carry

    lax.fori_loop(0, count // size, step, 0)


def shifted(rows, by):
    return pl.ds(aligned(rows.start + by, HEAD_DIM), rows.size)


def scale_rows(batch, tokens, gain, scaled, into=0):
    half = tokens.shape[1] // 2

    def body(rows):
        normed, _ = normalise(tokens[rows, :])
        values = (normed * gain[...]).astype(BF16)
        place = shifted(rows, into)
        scaled[place, :half] = jnp.where(batch == 0, values[:, :half], values[:, half:])
        scaled[place, half:] = jnp.where(batch == 0, values[:, half:], values[:, :half])

    over_rows(tokens.shape[0], body)


def norm_backward_rows(tokens, back, gain, out, at=0):
    def body(rows):
        place = shifted(rows, at)
        out[place, :] = norm_backward(tokens[rows, :], back[place, :], gain[...])

    over_rows(tokens.shape[0], body)


def times_rows(batch, left, weights, out, rows, chunk):
    half = weights.shape[0] // 2
    per_half = half // chunk

    def columns(index, carry):
        place = jnp.where(index < per_half, batch, 1 - batch) * half + lax.rem(index, per_half) * chunk
        product = dot(left(), weights[span(index * chunk, chunk), :], 1, 1)
        out[rows, span(place, chunk)] = product.astype(out.dtype)
        return carry

    lax.fori_loop(0, 2 * per_half, columns, 0)


def times_halves(batch, left, rows, weights, out, chunk):
    half = weights.shape[0] // 2

    def columns(index, carry):
        at = span(index * chunk, chunk)
        product = dot(left[rows, span(batch * half, half)], weights[:half, at], 1, 0)
        product = product + dot(left[rows, span((1 - batch) * half, half)], weights[half:, at], 1, 0)
        out[:, at] = product.astype(BF16)
        return carry

    lax.fori_loop(0, weights.shape[1] // chunk, columns, 0)


def weight_rows(here, there, full, sems):
    half = here.shape[0]
    size = half // PIECES
    return tuple(
        pltpu.make_async_copy(
            source.at[pl.ds(piece * size, size)],
            full.at[pl.ds(place * half + piece * size, size)],
            sems.at[place * PIECES + piece],
        )
        for place, source in enumerate((here, there))
        for piece in range(PIECES)
    )


def multiply_columns(tokens, weights, out):
    def columns(index, carry):
        at = span(index * QUAD, QUAD)
        out[:, at] = dot(tokens[...], weights[at, :], 1, 1).astype(BF16)
        return carry

    lax.fori_loop(0, weights.shape[0] // QUAD, columns, 0)


def own_kernel(meta, tokens, cot, gain, o_here, scaled, upstream, *sent):
    scale_rows(meta[BATCH], tokens, gain, scaled)
    multiply_columns(cot, o_here, upstream)
    near = meta[SLOT] == 0

    def cut(source, out, if_near, if_far):
        start = aligned(jnp.where(near, if_near, if_far) * HEAD_DIM, HEAD_DIM)
        out[...] = source[pl.ds(start, out.shape[0]), :]

    for index, count in enumerate(COUNTS):
        cut(tokens, sent[2 * index], LEAD, WIN - count)
        cut(cot, sent[2 * index + 1], 0, WIN - count)


def own_tokens(meta, tokens, cot, gain, o_here):
    rows, channels = tokens.shape
    half = o_here.shape[0]
    shapes = [(rows, channels), (rows, half)]
    for count in COUNTS:
        shapes += [((count - LEAD) * HEAD_DIM, channels), (count * HEAD_DIM, channels)]
    return call(
        own_kernel,
        "own_tokens",
        [SCALAR] + [VECTOR] * 4,
        [VECTOR] * len(shapes),
        [jax.ShapeDtypeStruct(shape, BF16) for shape in shapes],
        [],
        rows * channels * channels,
    )(meta, tokens, cot, gain, o_here)


def rest_kernel(
    meta, x_first, gain, scaled_in, cot_in, w_here, w_there, o_here, o_there, qkv, upstream, w_full, o_full,
    scaled, cot, sems, w_sems, o_sems,
):
    half, width = w_here.shape
    rows = qkv.shape[0]
    first = pl.ds(aligned(meta[FIRST], HEAD_DIM), x_first.shape[0])
    chunk = 1024
    chunks = width // chunk
    scaled_copy = pltpu.make_async_copy(scaled_in, scaled.at[pl.ds(0, rows)], sems.at[0])
    later = (pltpu.make_async_copy(cot_in, cot, sems.at[1]),) + weight_rows(o_here, o_there, o_full, o_sems)

    def weight_copies(index):
        at = pl.ds(aligned(index * chunk, chunk), chunk)
        return (
            pltpu.make_async_copy(w_here.at[:, at], w_full.at[pl.ds(0, half), at], w_sems.at[0, index]),
            pltpu.make_async_copy(w_there.at[:, at], w_full.at[pl.ds(half, half), at], w_sems.at[1, index]),
        )

    scaled_copy.start()

    def start_weights(index, carry):
        for copy in weight_copies(index):
            copy.start()
        return carry

    lax.fori_loop(0, chunks, start_weights, 0)
    for copy in later:
        copy.start()
    scale_rows(meta[BATCH], x_first, gain, scaled, rows)
    scaled_copy.wait()

    def project(index, carry):
        for copy in weight_copies(index):
            copy.wait()
        at = pl.ds(aligned(index * chunk, chunk), chunk)
        product = dot(scaled[...], w_full[:, at], 1, 0).astype(BF16)
        qkv[:, at] = product[:rows]
        qkv[first, at] = product[rows:]
        return carry

    lax.fori_loop(0, chunks, project, 0)
    for copy in later:
        copy.wait()
    multiply_columns(cot, o_full.at[pl.ds(half, half)], upstream)


def rest_projection(meta, x_first, gain, scaled, cot, w_here, w_there, o_here, o_there):
    rows, channels = scaled.shape
    half, width = w_there.shape
    shapes = [(rows, width), (rows, half), (channels, width), (channels, channels)]
    return call(
        rest_kernel,
        "rest_projection",
        [SCALAR] + [VECTOR] * 2 + [ANYWHERE] * 6,
        [VECTOR] * 4,
        [jax.ShapeDtypeStruct(shape, BF16) for shape in shapes],
        [
            pltpu.VMEM((rows + x_first.shape[0], channels), BF16),
            pltpu.VMEM((rows, channels), BF16),
            pltpu.SemaphoreType.DMA((2,)),
            pltpu.SemaphoreType.DMA((2, width // 1024)),
            pltpu.SemaphoreType.DMA((2 * PIECES,)),
        ],
        rows * channels * (2 * width + channels),
    )(meta, x_first, gain, scaled, cot, w_here, w_there, o_here, o_there)


def forward_kernel(
    meta, x_others, gain, qkv_in, w_full, o_full,
    update_out, qkv, raised_out, inverse_out, attended,
    scaled, scores_a, scores_b, peak_a, peak_b, low_a, low_b, values_t, outs_t,
):
    batch = meta[BATCH]
    channels, width = w_full.shape
    rows = qkv.shape[0]
    count = update_out.shape[0]
    slot = pl.ds(aligned(meta[SLOT], HEAD_DIM), count)
    others = pl.ds(aligned(meta[OTHERS], HEAD_DIM), scaled.shape[0])
    extra = pl.ds(aligned(meta[EXTRA], HEAD_DIM), HEAD_DIM)
    chunk = 512
    scale_rows(batch, x_others, gain, scaled)

    def project(index, carry):
        at = span(index * chunk, chunk)
        own = qkv[extra, at]
        qkv[others, at] = dot(scaled[...], w_full[:, at], 1, 0).astype(BF16)

        @pl.when(meta[ODD] == 1)
        def _():
            qkv[extra, at] = own

        return carry

    lax.fori_loop(0, width // chunk, project, 0)

    def columns(part, pair):
        return span(part * channels + pair * PAIR, PAIR)

    def scores(pair, head, out, peak):
        query = qkv[:, columns(0, pair)] * BF16(HEAD_DIM ** -0.5)
        values = dot(qkv[:, columns(1, pair)], head_mask(query, head), 1, 1)
        out[...] = values
        peak[...] = jnp.max(values, axis=0, keepdims=True)

    def softmax(head, source, peak, low):
        top = peak[...]
        sums = jnp.zeros((8, rows), F32)
        for at in range(0, rows, FEW_ROWS):
            raised = jnp.exp(source[pl.ds(at, FEW_ROWS), :] - top)
            raised_out[head, pl.ds(at, FEW_ROWS), :] = raised
            sums = sums + jnp.sum(raised.reshape(FEW_ROWS // 8, 8, rows), axis=0)
        inverse = 1.0 / jnp.sum(sums, axis=0, keepdims=True)
        inverse_out[head] = inverse
        for at in range(0, rows, FEW_ROWS):
            low[pl.ds(at, FEW_ROWS), :] = (raised_out[head, pl.ds(at, FEW_ROWS), :] * inverse).astype(BF16)

    pairs = channels // PAIR
    scores(0, 0, scores_a, peak_a)

    def pair_of_heads(pair, carry):
        before = jnp.maximum(pair - 1, 0)
        after = jnp.minimum(pair + 1, pairs - 1)
        outs_t[HEAD_DIM:] = dot(values_t[HEAD_DIM:], low_b[...], 1, 0).astype(BF16)
        attended[:, columns(0, before)] = outs_t[...].T
        scores(pair, 1, scores_b, peak_b)
        softmax(2 * pair, scores_a, peak_a, low_a)
        values_t[...] = qkv[:, columns(2, pair)].T
        outs_t[:HEAD_DIM] = dot(values_t[:HEAD_DIM], low_a[...], 1, 0).astype(BF16)
        scores(after, 0, scores_a, peak_a)
        softmax(2 * pair + 1, scores_b, peak_b, low_b)
        return carry

    lax.fori_loop(0, pairs, pair_of_heads, 0, unroll=PAIRS_AT_ONCE)
    outs_t[HEAD_DIM:] = dot(values_t[HEAD_DIM:], low_b[...], 1, 0).astype(BF16)
    attended[:, columns(0, pairs - 1)] = outs_t[...].T
    times_halves(batch, attended, slot, o_full, update_out, chunk)


def forward(meta, x_others, gain, qkv, w_full, o_full):
    rows, width = qkv.shape
    channels = width // 3
    count = x_others.shape[0] + LEAD * HEAD_DIM
    heads = channels // HEAD_DIM
    return call(
        forward_kernel,
        "forward",
        [SCALAR] + [VECTOR] * 5,
        [VECTOR] * 5,
        [
            jax.ShapeDtypeStruct((count, channels), BF16),
            jax.ShapeDtypeStruct((rows, width), BF16),
            jax.ShapeDtypeStruct((heads, rows, rows), F32),
            jax.ShapeDtypeStruct((heads, 1, rows), F32),
            jax.ShapeDtypeStruct((rows, channels), BF16),
        ],
        [
            pltpu.VMEM(x_others.shape, BF16),
            pltpu.VMEM((rows, rows), F32),
            pltpu.VMEM((rows, rows), F32),
            pltpu.VMEM((1, rows), F32),
            pltpu.VMEM((1, rows), F32),
            pltpu.VMEM((rows, rows), BF16),
            pltpu.VMEM((rows, rows), BF16),
            pltpu.VMEM((PAIR, rows), BF16),
            pltpu.VMEM((PAIR, rows), BF16),
        ],
        12 * 10 ** 9,
        aliases={3: 1},
    )(meta, x_others, gain, qkv, w_full, o_full)


def backward_kernel(meta, *refs, width, begins, ends):
    refs = list(refs)

    def take(count):
        taken = refs[:count]
        del refs[:count]
        return taken

    qkv, raised, inverse, u_here, u_there = take(5)
    if not begins:
        dk_before, dv_before, _ = take(3)
    if ends:
        x_first, x_others, c_slot, gain, w_full, o_full = take(6)
        (grad_out,) = take(1)
    else:
        dk_out, dv_out = take(2)
    (
        grad_qkv,
        upstream, grads_a, grads_b, sum_a, sum_b, scores_a, scores_b, low_a, low_b, keys_t, dq_t, dk_sum, dv_sum,
    ) = take(14)
    batch = meta[BATCH]
    rows = qkv.shape[0]
    half = u_here.shape[1]
    channels = 2 * half
    slot_start = meta[SLOT]
    if width == rows:
        start = 0
    else:
        start = jnp.where((slot_start == 0) == ends, 0, width)
    tokens = pl.ds(aligned(start, width), width)
    here, there = span(batch * half, half), span((1 - batch) * half, half)
    upstream[:, here] = u_here[tokens, :]
    upstream[:, there] = u_there[tokens, :]

    if ends:
        count = c_slot.shape[0]
        place = pl.ds(aligned(slot_start - start, HEAD_DIM), count)
        times_rows(batch, lambda: c_slot[...], o_full, upstream, place, 2 * QUAD)

        @pl.when(meta[ODD] == 1)
        def _():
            local = pl.ds(aligned(meta[EXTRA] - start, HEAD_DIM), HEAD_DIM)
            extra = pl.ds(aligned(meta[EXTRA], HEAD_DIM), HEAD_DIM)
            upstream[local, here] = u_here[extra, :]
            upstream[local, there] = u_there[extra, :]

    def columns(part, pair):
        return span(part * channels + pair * PAIR, PAIR)

    def grad_probs(pair, head, out, row_sum):
        values = head_mask(qkv[:, columns(2, pair)], head)
        grads = dot(values, upstream[:, columns(0, pair)], 1, 1)
        out[...] = grads
        index = 2 * pair + head
        row_sum[...] = jnp.sum(grads * raised[index, :, tokens], axis=0, keepdims=True) * inverse[index, :, tokens]

    def score_grads(head, source, row_sum, scores, low):
        total = row_sum[...]
        scale = inverse[head, :, tokens]
        for at in range(0, rows, ROW_CHUNK):
            part = pl.ds(at, ROW_CHUNK)
            soft = raised[head, part, tokens] * scale
            low[part, :] = soft.astype(BF16)
            scores[part, :] = (soft * (source[part, :] - total)).astype(BF16)

    def products(pair, head, scores, low):
        from_keys = dot(scores[...], head_mask(qkv[tokens, columns(0, pair)], head), 1, 0)
        from_values = dot(low[...], head_mask(upstream[:, columns(0, pair)], head), 1, 0)
        part = slice(HEAD_DIM * head, HEAD_DIM * head + HEAD_DIM)
        dq_t[part] = (dot(keys_t[part], scores[...], 1, 0) * HEAD_DIM ** -0.5).astype(BF16)
        if head == 0:
            dk_sum[...] = from_keys
            dv_sum[...] = from_values
            return
        from_keys = dk_sum[...] + from_keys
        from_values = dv_sum[...] + from_values
        at = columns(0, pair)
        grad_qkv[tokens, at] = dq_t[...].T
        if not begins:
            from_keys = dk_before[:, at] + from_keys
            from_values = dv_before[:, at] + from_values
        if ends:
            grad_qkv[:, columns(1, pair)] = (from_keys * HEAD_DIM ** -0.5).astype(BF16)
            grad_qkv[:, columns(2, pair)] = from_values.astype(BF16)
        else:
            dk_out[:, at] = from_keys
            dv_out[:, at] = from_values

    pairs = channels // PAIR
    grad_probs(0, 0, grads_a, sum_a)

    def pair_of_heads(pair, carry):
        before = jnp.maximum(pair - 1, 0)
        after = jnp.minimum(pair + 1, pairs - 1)
        products(before, 1, scores_b, low_b)
        grad_probs(pair, 1, grads_b, sum_b)
        score_grads(2 * pair, grads_a, sum_a, scores_a, low_a)
        keys_t[...] = qkv[:, columns(1, pair)].T
        products(pair, 0, scores_a, low_a)
        grad_probs(after, 0, grads_a, sum_a)
        score_grads(2 * pair + 1, grads_b, sum_b, scores_b, low_b)
        return carry

    lax.fori_loop(0, pairs, pair_of_heads, 0, unroll=PAIRS_AT_ONCE)
    products(pairs - 1, 1, scores_b, low_b)
    if ends:
        back, x_slot = take(2)
        slot = pl.ds(aligned(slot_start, HEAD_DIM), count)
        for part, at in zip((x_first, x_others), (FIRST, OTHERS)):
            x_slot[pl.ds(aligned(meta[at] - slot_start, HEAD_DIM), part.shape[0]), :] = part[...]
        times_rows(batch, lambda: grad_qkv[slot, :], w_full, back, slice(None), 2 * QUAD)
        norm_backward_rows(x_slot, back, gain, grad_out)


def backward(meta, window, before=None, received=None, half=False):
    rows, width = window[0].shape
    channels = width // 3
    tokens = rows // 2 if half else rows
    begins, ends = before is None, received is not None
    square = (rows, tokens)
    operands = list(window) + list(before or ()) + list(received or ())
    sums = jax.ShapeDtypeStruct((rows, channels), F32)
    results = [jax.ShapeDtypeStruct((rows, width), BF16)]
    scratch = [
        pltpu.VMEM((tokens, channels), BF16),
        pltpu.VMEM(square, F32),
        pltpu.VMEM(square, F32),
        pltpu.VMEM((1, tokens), F32),
        pltpu.VMEM((1, tokens), F32),
        pltpu.VMEM(square, BF16),
        pltpu.VMEM(square, BF16),
        pltpu.VMEM(square, BF16),
        pltpu.VMEM(square, BF16),
        pltpu.VMEM((PAIR, rows), BF16),
        pltpu.VMEM((PAIR, tokens), BF16),
        pltpu.VMEM((rows, PAIR), F32),
        pltpu.VMEM((rows, PAIR), F32),
    ]
    if ends:
        count = received[2].shape[0]
        results = [jax.ShapeDtypeStruct((count, channels), BF16)] + results
        scratch = scratch + [pltpu.VMEM((count, channels), F32), pltpu.VMEM((count, channels), BF16)]
    else:
        results = [sums, sums] + results
    return call(
        functools.partial(backward_kernel, width=tokens, begins=begins, ends=ends),
        "backward",
        [SCALAR] + [VECTOR] * len(operands),
        [VECTOR] * len(results),
        results,
        scratch,
        (10 if half else 20) * 10 ** 9,
        aliases=None if begins else {len(window) + len(before): len(results) - 1},
    )(meta, *operands)


def finish_kernel(
    meta, tokens, gain, attended, grad_qkv, received, w_full, o_full, update_out, grad_out,
    update, grad, back, sems,
):
    batch = meta[BATCH]
    rows, channels = tokens.shape
    count = received.shape[0]
    everything = slice(None)

    def copies(source, out, which):
        size = rows // PIECES
        return tuple(
            pltpu.make_async_copy(
                source.at[pl.ds(piece * size, size)], out.at[pl.ds(piece * size, size)], sems.at[which, piece]
            )
            for piece in range(PIECES)
        )

    times_halves(batch, attended, everything, o_full, update, 2 * QUAD)
    extra = pl.ds(aligned(meta[EXTRA], HEAD_DIM), HEAD_DIM)
    kept = update[extra, :]
    update[pl.ds(aligned(meta[SLOT], HEAD_DIM), count), :] = received[...]

    @pl.when(meta[ODD] == 1)
    def _():
        update[extra, :] = kept

    for copy in copies(update, update_out, 0):
        copy.start()
    times_rows(batch, lambda: grad_qkv[...], w_full, back, everything, 2 * QUAD)
    norm_backward_rows(tokens, back, gain, grad)
    for copy in copies(grad, grad_out, 1):
        copy.start()
    for copy in copies(update, update_out, 0) + copies(grad, grad_out, 1):
        copy.wait()


def finish(meta, tokens, gain, attended, grad_qkv, received, w_full, o_full):
    rows, channels = tokens.shape
    block = jax.ShapeDtypeStruct((rows, channels), BF16)
    return call(
        finish_kernel,
        "finish",
        [SCALAR] + [VECTOR] * 7,
        [ANYWHERE] * 2,
        [block] * 2,
        [
            pltpu.VMEM((rows, channels), BF16),
            pltpu.VMEM((rows, channels), BF16),
            pltpu.VMEM((rows, channels), F32),
            pltpu.SemaphoreType.DMA((2, PIECES)),
        ],
        8 * rows * channels * channels,
    )(meta, tokens, gain, attended, grad_qkv, received, w_full, o_full)


def merge_kernel(meta, grad_back, grad, out, sems):
    for index in range(grad_back.shape[0] // HEAD_DIM):
        start = aligned(meta[SLOT] + index * HEAD_DIM, HEAD_DIM)
        copy = pltpu.make_async_copy(
            grad_back.at[pl.ds(index * HEAD_DIM, HEAD_DIM)], out.at[pl.ds(start, HEAD_DIM)], sems.at[index]
        )
        wanted = jnp.logical_not((meta[ODD] == 1) & (start == meta[EXTRA]))
        pl.when(wanted)(copy.start)

    for index in range(grad_back.shape[0] // HEAD_DIM):
        start = aligned(meta[SLOT] + index * HEAD_DIM, HEAD_DIM)
        copy = pltpu.make_async_copy(
            grad_back.at[pl.ds(index * HEAD_DIM, HEAD_DIM)], out.at[pl.ds(start, HEAD_DIM)], sems.at[index]
        )
        wanted = jnp.logical_not((meta[ODD] == 1) & (start == meta[EXTRA]))
        pl.when(wanted)(copy.wait)


def merge(meta, grad_back, grad):
    return call(
        merge_kernel, "merge", [SCALAR, VECTOR, ANYWHERE], ANYWHERE, jax.ShapeDtypeStruct(grad.shape, BF16),
        [pltpu.SemaphoreType.DMA((HALF_WIN,))], 0, aliases={2: 0},
    )(meta, grad_back, grad)


def after_kernel(rows, earlier, out):
    pass


def after(rows, earlier):
    return call(
        after_kernel, "after", [ANYWHERE] * 2, ANYWHERE, jax.ShapeDtypeStruct(rows.shape, BF16), [], 0,
        aliases={0: 0},
    )(rows, earlier)


def exchange(rows, near, back):
    size = lax.axis_size("space")

    def along(by):
        return lax.ppermute(rows, "space", [(i, (i + by) % size) for i in range(size)])

    if size == 2 * YTILES:
        return along(YTILES)
    return jnp.where(near != back, along(-YTILES), along(YTILES))


def swapped(part):
    return lax.ppermute(part, "batch", [(0, 1), (1, 0)])


def shards(inputs, cotangent, offsets, w_qkv, w_out, gain):
    tiled_shape = inputs.shape
    channels = tiled_shape[-1]
    row = WIN * tiled_shape[4]
    tokens = inputs.reshape(-1, channels)
    cot = cotangent.reshape(-1, channels)
    gain = gain.reshape(1, channels)
    shift = offsets[0]
    near = shift <= HALF_WIN
    moved = jnp.minimum(shift, WIN - shift)
    batch = lax.axis_index("batch")

    first = jnp.where(near, 0, (WIN - LEAD) * row)
    o_there = swapped(w_out)
    w_there = swapped(w_qkv)
    x_first = exchange(lax.dynamic_slice_in_dim(tokens, first, LEAD * row, 0), near, False)

    def meta_of(count):
        slot = jnp.where(near, 0, (WIN - count) * row)
        others = jnp.where(near, LEAD * row, (WIN - count) * row)
        extra = jnp.where(near, (count - 1) * row, (WIN - count) * row)
        return jnp.stack([batch, slot, first, others, extra, moved < count]).astype(jnp.int32)

    scaled, u_here, *sent = own_tokens(meta_of(COUNTS[0]), tokens, cot, gain, w_out)

    def branch(count):
        def run(tokens, cot, x_first, scaled, u_here, weights, sent):
            meta = meta_of(count)
            x_sent, c_sent = sent[2 * COUNTS.index(count) :][:2]
            x_others = exchange(x_sent, near, False)
            c_slot = exchange(after(c_sent, x_others), near, False)
            qkv, u_there, w_full, o_full = rest_projection(meta, x_first, gain, scaled, cot, *weights)
            update_sent, window, raised, inverse, attended = forward(meta, x_others, gain, qkv, w_full, o_full)
            window = (window, raised, inverse, u_here, u_there)
            received = (x_first, x_others, c_slot, gain, w_full, o_full)
            update_back = exchange(after(update_sent, c_slot), near, True)
            if count in HALVED:
                before = backward(meta, window, half=True)
                grad_sent, grad_qkv = backward(meta, window, before, received, half=True)
            else:
                grad_sent, grad_qkv = backward(meta, window, received=received)
            grad_back = exchange(grad_sent, near, True)
            update, grad = finish(meta, tokens, gain, attended, grad_qkv, update_back, w_full, o_full)
            return update, merge(meta, grad_back, grad)

        return run

    update, grad = lax.switch(
        jnp.maximum(moved, COUNTS[0]) - COUNTS[0],
        [branch(count) for count in COUNTS],
        tokens, cot, x_first, scaled, u_here, (w_qkv, w_there, w_out, o_there), tuple(sent),
    )
    return (update.reshape(tiled_shape), grad.reshape(tiled_shape))


def solution(mesh):
    in_specs = (
        P(("groups", "batch"), "space", None, None, None, None),
        P(("groups", "batch"), "space", None, None, None, None),
        P(("groups", "batch")),
        P("batch", None),
        P("batch", None),
        P(),
    )
    out_specs = (
        P(("groups", "batch"), "space", None, None, None, None),
        P(("groups", "batch"), "space", None, None, None, None),
    )
    return jax.shard_map(shards, mesh=mesh, in_specs=in_specs, out_specs=out_specs, check_vma=False)
```
